128 devices in a mesh: band: 16 (over z_lo, x, core), pw: 8 (over z_hi, y).
Axes of the slice: x: 4, y: 4, z: 4 (z_hi: 2, z_lo: 2; z = z_hi * 2 + z_lo), core: 2. Of those that a mesh axis runs over, the one named last changes fastest.
Arguments:
- wave_coeffs: bfloat16 [16, 2, 491520], P('band', None, 'pw'), may hold values from -6 to 6
- potential: float32 [96, 9216], P(None, 'pw'), may hold values from -1.5 to 3
- sphere_index: int32 [491520], P('pw'), may hold values from 0 to 884735, as said below
- rotation: float32 [16, 64], P('pw'), may hold values from -1.5 to 1.5
- panel_order: int32 [16], replicated, may hold values from 0 to 15, each once
Outputs:
- rotated: float32 [64, 2, 491520], P('band', None, 'pw')
The draws below stay inside these ranges and needn't reach their ends.
Inputs may be any that keep to these rules, and one draw needn't show every extreme that they name: `sphere_index`: all entries are distinct. The k-th run of 61440 entries is increasing and lies in the grid planes x = k * 12 to (k + 1) * 12 - 1, and holds the first and the last cell of those planes.
All inputs are finite; a program needn't handle non-finite values.
Results may differ from the reference program's by a relative error of at most 0.0003.
Values sent between devices are 32-bit elements; how exact they have to be, the bound alone decides.
A program may use at most 192 MiB of HBM per device.

```python
import math
import jax
import jax.numpy as jnp
from jax import lax

NG = 96
WIN_BANDS = 16
OUT_BANDS = 64
NPW = 491520
SLAB_PW = 61440
SLAB_X = 12
PANELS = 16
PANEL_ROWS = 1


def draw_sphere_index(key, part):
    slab_cells = NG * NG * SLAB_X

    def one_slab(slab_number):
        inner = jax.random.permutation(jax.random.fold_in(key, slab_number), slab_cells - 2)[:SLAB_PW - 2]
        inner = inner.astype(jnp.int32) + 1
        ends = jnp.array([0, slab_cells - 1], dtype=jnp.int32)
        chosen = jnp.sort(jnp.concatenate([ends, inner]))
        return chosen + slab_number * slab_cells
    return jax.vmap(one_slab)(jnp.arange(SLAB_X * 0 + NG // SLAB_X, dtype=jnp.int32)).reshape(-1)


def level_of(key, shape, pieces, least, largest):
    factor_of = 1.0
    for axis_at, parts in pieces:
        draws = jax.random.uniform(jax.random.fold_in(jax.random.fold_in(key, 6), axis_at), (parts,), jnp.float32, least / len(pieces), largest / len(pieces))
        factor_of = factor_of * jnp.repeat(jnp.exp(draws), shape[axis_at] // parts).reshape((-1,) + (1,) * (len(shape) - 1 - axis_at))
    return factor_of


def centred(key, extent, width, reach, split=(), kind=jnp.bfloat16):
    loudness = level_of(key, extent, split, -0.22, 0.18) if split else 1.0
    drawn = jax.random.normal(key, extent, jnp.float32) * width * loudness
    return jnp.minimum(jnp.maximum(drawn, -reach), reach).astype(kind)


def setup_inputs(seed: int = 0) -> dict:
    key_of = jax.random.split(jax.random.key(seed), 6)
    wave_coeffs = centred(key_of[0], (WIN_BANDS, 2, NPW), 1.0, 6.0, ((0, 16), (2, 8)))
    potential = jnp.clip(-1.5 + 4.5 * jax.random.uniform(key_of[1], (NG, NG * NG), jnp.float32) ** level_of(key_of[1], (NG, NG * NG), ((1, 8),), -0.2, 0.2), -1.5, 3.0)
    sphere_index = draw_sphere_index(jax.random.fold_in(key_of[5], 71), 0)
    rotation = centred(key_of[3], (WIN_BANDS, OUT_BANDS), WIN_BANDS ** -0.5, 1.5, ((0, 8),), jnp.float32)
    panel_order = jax.random.permutation(key_of[4], PANELS).astype(jnp.int32)
    return {"wave_coeffs": wave_coeffs, "potential": potential, "sphere_index": sphere_index, "rotation": rotation, "panel_order": panel_order}


HIGHEST = lax.Precision.HIGHEST

def dft_tables(length, direction):
    counter = jnp.arange(length, dtype=jnp.int32)
    products = counter[:, None] * counter[None, :] % length
    angles = 2.0 * math.pi / length * products.astype(jnp.float32)
    scaling = 1.0 / math.sqrt(length)
    cosines = jnp.cos(angles) * scaling
    sine_table = direction * jnp.sin(angles) * scaling
    upper = jnp.stack([cosines, -sine_table], axis=1)
    lower = jnp.stack([sine_table, cosines], axis=1)
    return jnp.stack([upper, lower], axis=0)

def along_axis(field, table, pattern):
    return jnp.einsum(pattern, table, field, precision=HIGHEST)

def signed_frequency(position):
    return jnp.where(position < NG // 2, position, position - NG).astype(jnp.float32)

def kinetic(sphere_index):
    plane_cells = NG * NG
    index_x = sphere_index // plane_cells
    index_y = sphere_index // NG % NG
    index_z = sphere_index % NG
    total = signed_frequency(index_x) ** 2 + signed_frequency(index_y) ** 2 + signed_frequency(index_z) ** 2
    return 2.0 * total / float((NG // 2) ** 2)

def reference(wave_coeffs, potential, sphere_index, rotation, panel_order):
    kinetic_term = kinetic(sphere_index)
    inverse = dft_tables(NG, 1.0)
    forward = dft_tables(NG, -1.0)
    potential_grid = potential.reshape(NG, NG, NG)

    def one_band(coeffs):
        values = coeffs.astype(jnp.float32)
        field = jnp.zeros((2, NG * NG * NG), jnp.float32).at[:, sphere_index].set(values).reshape(2, NG, NG, NG)
        for pattern in ('okcn,cxyn->oxyk', 'okcn,cxnz->oxkz', 'okcn,cnyz->okyz'):
            field = along_axis(field, inverse, pattern)
        field = potential_grid[None] * field
        for pattern in ('okcn,cnyz->okyz', 'okcn,cxnz->oxkz', 'okcn,cxyn->oxyk'):
            field = along_axis(field, forward, pattern)
        back = field.reshape(2, -1)[:, sphere_index]
        return kinetic_term[None] * values + back
    applied = lax.map(one_band, wave_coeffs)
    ordered = rotation.reshape(PANELS, PANEL_ROWS, OUT_BANDS)[panel_order].reshape(WIN_BANDS, OUT_BANDS)
    return jnp.einsum('ij,icg->jcg', ordered, applied, precision=HIGHEST)
```

```python
import math

import jax
import jax.numpy as jnp
import numpy as np
from jax import lax
from jax.experimental import pallas as pl
from jax.experimental.pallas import tpu as pltpu
from jax.sharding import PartitionSpec as P
import ml_dtypes

NG = 96
PARTS = 8
PLANES = NG // PARTS
GRID_ROWS = PLANES * NG
PIECE = PLANES * PLANES
PACKED = 480
CHIPS = 8
CHUNK = 2 * PACKED // CHIPS
BANDS = 16
OUT_LOCAL = 4
GUARD = 512
BLOCK = 48
FLAG = 1 << 20
MESH = pl.DeviceIdType.MESH
VMEM_SPEC = pl.BlockSpec(memory_space=pltpu.VMEM)
SMEM_SPEC = pl.BlockSpec(memory_space=pltpu.SMEM)
VMEM_BYTES = 48 * 1024 * 1024


def split_table(table):
    high = table.astype(ml_dtypes.bfloat16)
    low = (table - high.astype(np.float64)).astype(ml_dtypes.bfloat16)
    return np.stack([high, low])


def tables(direction):
    counter = np.arange(NG)
    angles = 2.0 * math.pi / NG * (np.outer(counter, counter) % NG)
    cosines = np.cos(angles) / math.sqrt(NG)
    sines = direction * np.sin(angles) / math.sqrt(NG)
    right = np.zeros((256, 256))
    right[:NG, :NG] = cosines
    right[128 : 128 + NG, :NG] = -sines
    right[:NG, 128 : 128 + NG] = sines
    right[128 : 128 + NG, 128 : 128 + NG] = cosines
    left = np.concatenate([cosines, sines], axis=0)
    padded = np.zeros((2, PARTS, 16, NG))
    padded[:, :, :PLANES] = left.reshape(2, PARTS, PLANES, NG)
    return split_table(right), split_table(left), split_table(padded.reshape(256, NG))


def split(value):
    high = value.astype(jnp.bfloat16)
    return high, (value - high.astype(jnp.float32)).astype(jnp.bfloat16)


def dot(a, b):
    return jnp.dot(a, b, preferred_element_type=jnp.float32)


def left_transform(table_ref, field):
    high, low = split(field)
    product = dot(table_ref[0], high) + dot(table_ref[0], low) + dot(table_ref[1], high)
    half = product.shape[0] // 2
    real = product[:half, :128] - product[half:, 128:]
    imag = product[:half, 128:] + product[half:, :128]
    return real, imag


def right_transform(table_ref, field):
    high, low = split(field)
    return dot(high, table_ref[0]) + dot(low, table_ref[0]) + dot(high, table_ref[1])


def cell_of(index):
    line = ((index.astype(jnp.float32) + 0.5) * (1.0 / NG)).astype(jnp.int32)
    return line, index - NG * line


def spread_kernel(index_ref, wave_ref, right_ref, padded_ref, real_ref, imag_ref, gap_ref, vr, vi, gap):
    first_line = lax.axis_index("pw") * GRID_ROWS
    lane = lax.broadcasted_iota(jnp.int32, (BLOCK, 128), 1)
    rows = lax.broadcasted_iota(jnp.int32, (BLOCK, 128), 0)
    zero = jnp.zeros((BLOCK, 128), jnp.float32)
    total = GUARD + GRID_ROWS

    def clear(step, carry):
        at = pl.ds(pl.multiple_of(step * 64, 64), 64)
        vr[at, :] = jnp.zeros((64, 128), jnp.float32)
        vi[at, :] = jnp.zeros((64, 128), jnp.float32)
        gap[at, :] = jnp.zeros((64, 128), jnp.int32)
        return carry

    lax.fori_loop(0, total // 64, clear, 0)

    def place(step, carry):
        base = pl.multiple_of(step * BLOCK, BLOCK)
        line, z = cell_of(index_ref[pl.ds(base, BLOCK), :])
        position = (rows + base) * 128 + lane
        at = pl.ds(pl.multiple_of(GUARD + base, 16), BLOCK)
        gap[at, :] = ((line - first_line) * 128 + z - position) | FLAG
        vr[at, :] = wave_ref[pl.ds(2 * base, BLOCK, stride=2), :]
        vi[at, :] = wave_ref[pl.ds(2 * base + 1, BLOCK, stride=2), :]
        return carry

    lax.fori_loop(0, PACKED // BLOCK, place, 0)

    steps = GRID_ROWS // BLOCK
    for bit in range(16, -1, -1):
        shift = 1 << bit

        def move(step, carry, shift=shift):
            base = GUARD + (steps - 1 - step) * BLOCK
            here = pl.ds(pl.multiple_of(base, 16), BLOCK)
            if shift >= 128:
                there = pl.ds(base - shift // 128, BLOCK)
            else:
                there = pl.ds(base - 1, BLOCK)
            own = [ref[here, :] for ref in (gap, vr, vi)]
            other = [ref[there, :] for ref in (gap, vr, vi)]
            if shift < 128:
                stay = lane < 128 - shift
                other = [pltpu.roll(jnp.where(stay, a, b), shift, 1) for a, b in zip(own, other)]
            arrives = (other[0] & shift) != 0
            left = jnp.where((own[0] & shift) != 0, 0, own[0])
            gap[here, :] = jnp.where(arrives, other[0], left)
            vr[here, :] = jnp.where(arrives, other[1], own[1])
            vi[here, :] = jnp.where(arrives, other[2], own[2])
            return carry

        lax.fori_loop(0, steps, move, 0)

    for x in range(PLANES):
        at = pl.ds(GUARD + x * NG, NG)
        held = gap[at, :]
        gap_ref[pl.ds(x * NG, NG), :] = held
        filled = (held & FLAG) != 0
        field = jnp.concatenate(
            [jnp.where(filled, vr[at, :], 0.0), jnp.where(filled, vi[at, :], 0.0)], axis=1
        ).astype(jnp.bfloat16)
        field = dot(field, right_ref[0]) + dot(field, right_ref[1])
        real, imag = left_transform(padded_ref, field)
        for d in range(PARTS):
            at = pl.ds(d * PIECE + x * PLANES, PLANES)
            real_ref[at, :] = real[16 * d : 16 * d + PLANES]
            imag_ref[at, :] = imag[16 * d : 16 * d + PLANES]


def lines_kernel(
    send_real, send_imag, potential_ref, rotation_ref, inverse_ref, forward_ref,
    out_real, out_imag, rotations,
    got_real, got_imag, back_real, back_imag, send_sem, recv_sem, own_sem,
):
    me = lax.axis_index("pw")
    barrier = pltpu.get_barrier_semaphore()
    for turn in range(1, PARTS):
        pl.semaphore_signal(
            barrier, inc=1, device_id={"pw": lax.rem(me + turn, PARTS)}, device_id_type=MESH
        )
    pl.semaphore_wait(barrier, PARTS - 1)

    def piece(ref, which):
        return ref.at[pl.ds(pl.multiple_of(which * PIECE, PIECE), PIECE), :]

    def exchange(phase, sources, targets):
        copies = []
        for turn in range(1, PARTS):
            peer = lax.rem(me + turn, PARTS)
            for part, (source, target) in enumerate(zip(sources, targets)):
                copy = pltpu.make_async_remote_copy(
                    src_ref=piece(source, peer),
                    dst_ref=piece(target, me),
                    send_sem=send_sem.at[phase, part, turn],
                    recv_sem=recv_sem.at[phase, part, turn],
                    device_id={"pw": peer},
                    device_id_type=MESH,
                )
                copy.start()
                copies.append(copy)
        for part, (source, target) in enumerate(zip(sources, targets)):
            copy = pltpu.make_async_copy(piece(source, me), piece(target, me), own_sem.at[phase, part])
            copy.start()
            copies.append(copy)
        return copies

    small = []
    for turn in range(1, PARTS):
        copy = pltpu.make_async_remote_copy(
            src_ref=rotation_ref,
            dst_ref=rotations.at[me],
            send_sem=send_sem.at[2, 0, turn],
            recv_sem=recv_sem.at[2, 0, turn],
            device_id={"pw": lax.rem(me + turn, PARTS)},
            device_id_type=MESH,
        )
        copy.start()
        small.append(copy)
    copy = pltpu.make_async_copy(rotation_ref, rotations.at[me], own_sem.at[2, 0])
    copy.start()
    small.append(copy)

    first = exchange(0, (send_real, send_imag), (got_real, got_imag))
    for copy in first:
        copy.wait()
    for b in range(PLANES):
        column = pl.ds(b, NG, stride=PLANES)
        field = jnp.concatenate([got_real[column, :], got_imag[column, :]], axis=1)
        real, imag = left_transform(inverse_ref, field)
        offset = b * NG % 128
        start = b * NG - offset
        if offset + NG > 128:
            local = pltpu.roll(potential_ref[:, start : start + 256], 256 - offset, 1)[:, :128]
        else:
            local = potential_ref[:, start : start + 128]
            if offset:
                local = pltpu.roll(local, 128 - offset, 1)
        field = jnp.concatenate([local * real, local * imag], axis=1)
        real, imag = left_transform(forward_ref, field)
        back_real[column, :] = real
        back_imag[column, :] = imag
    second = exchange(1, (back_real, back_imag), (out_real, out_imag))
    for copy in second + small:
        copy.wait()


def pick_kernel(
    back_real, back_imag, gap_ref, wave_ref, index_ref, left_ref, right_ref, applied_ref,
    plane_real, plane_imag, vr, vi, gap,
):
    lane = lax.broadcasted_iota(jnp.int32, (BLOCK, 128), 1)
    for x in range(PLANES):
        for d in range(PARTS):
            source = pl.ds(d * PIECE + x * PLANES, PLANES)
            target = pl.ds(d * PLANES, PLANES)
            plane_real[x, target, :] = back_real[source, :]
            plane_imag[x, target, :] = back_imag[source, :]
        field = jnp.concatenate([plane_real[x], plane_imag[x]], axis=1)
        real, imag = left_transform(left_ref, field)
        field = right_transform(right_ref, jnp.concatenate([real, imag], axis=1))
        at = pl.ds(x * NG, NG)
        vr[at, :] = field[:, :128]
        vi[at, :] = field[:, 128:]
        gap[at, :] = gap_ref[at, :]

    def clear(step, carry):
        at = pl.ds(pl.multiple_of(GRID_ROWS + step * 64, 64), 64)
        gap[at, :] = jnp.zeros((64, 128), jnp.int32)
        vr[at, :] = jnp.zeros((64, 128), jnp.float32)
        vi[at, :] = jnp.zeros((64, 128), jnp.float32)
        return carry

    lax.fori_loop(0, GUARD // 64, clear, 0)
    steps = GRID_ROWS // BLOCK
    for bit in range(17):
        shift = 1 << bit

        def move(step, carry, shift=shift):
            base = step * BLOCK
            here = pl.ds(pl.multiple_of(base, 16), BLOCK)
            if shift >= 128:
                there = pl.ds(base + shift // 128, BLOCK)
            else:
                there = pl.ds(base + 1, BLOCK)
            own = [ref[here, :] for ref in (gap, vr, vi)]
            other = [ref[there, :] for ref in (gap, vr, vi)]
            if shift < 128:
                stay = lane >= shift
                other = [pltpu.roll(jnp.where(stay, a, b), 128 - shift, 1) for a, b in zip(own, other)]
            arrives = (other[0] & shift) != 0
            left = jnp.where((own[0] & shift) != 0, 0, own[0])
            gap[here, :] = jnp.where(arrives, other[0], left)
            vr[here, :] = jnp.where(arrives, other[1], own[1])
            vi[here, :] = jnp.where(arrives, other[2], own[2])
            return carry

        lax.fori_loop(0, steps, move, 0)

    def signed_square(position):
        signed = jnp.where(position < NG // 2, position, position - NG).astype(jnp.float32)
        return signed * signed

    def finish(step, carry):
        base = pl.multiple_of(step * BLOCK, BLOCK)
        line, z = cell_of(index_ref[pl.ds(base, BLOCK), :])
        x, y = cell_of(line)
        energy = 2.0 * (signed_square(x) + signed_square(y) + signed_square(z)) / float((NG // 2) ** 2)
        for part, ref in enumerate((vr, vi)):
            at = pl.ds(2 * base + part, BLOCK, stride=2)
            applied_ref[at, :] = energy * wave_ref[at, :] + ref[pl.ds(base, BLOCK), :]
        return carry

    lax.fori_loop(0, PACKED // BLOCK, finish, 0)


def rotate_kernel(
    applied_ref, rotations, order_ref, out_ref,
    window, mixed, send_sem, recv_sem, pair_send, pair_recv, own_sem,
):
    band = lax.axis_index("band")
    chip, core = band // 2, band % 2
    sibling = {"band": chip * 2 + 1 - core}
    barrier = pltpu.get_barrier_semaphore()
    pl.semaphore_signal(barrier, inc=1, device_id=sibling, device_id_type=MESH)
    for turn in range(1, CHIPS):
        peer = lax.rem(chip + turn, CHIPS)
        pl.semaphore_signal(barrier, inc=1, device_id={"band": peer * 2 + core}, device_id_type=MESH)
    pl.semaphore_wait(barrier, CHIPS)

    def rows(which):
        return pl.ds(pl.multiple_of(which * CHUNK, CHUNK), CHUNK)

    own = pltpu.make_async_copy(applied_ref.at[rows(chip), :], window.at[band], own_sem.at[0])
    own.start()
    sent = []
    for turn in range(1, CHIPS):
        peer = lax.rem(chip + turn, CHIPS)
        copy = pltpu.make_async_remote_copy(
            src_ref=applied_ref.at[rows(peer), :],
            dst_ref=window.at[band],
            send_sem=send_sem.at[0, turn],
            recv_sem=recv_sem.at[0, turn],
            device_id={"band": peer * 2 + core},
            device_id_type=MESH,
        )
        copy.start()
        sent.append(copy)

    pairs = []

    def pass_on(source, turn):
        copy = pltpu.make_async_remote_copy(
            src_ref=window.at[source],
            dst_ref=window.at[source],
            send_sem=pair_send.at[turn],
            recv_sem=pair_recv.at[turn],
            device_id=sibling,
            device_id_type=MESH,
        )
        copy.start()
        pairs.append(copy)

    own.wait()
    pass_on(band, 0)
    for turn in range(1, CHIPS):
        sent[turn - 1].wait_recv()
        pass_on(lax.rem(chip - turn + CHIPS, CHIPS) * 2 + core, turn)
    for copy in pairs:
        copy.wait()
    for copy in sent:
        copy.wait_send()

    results = []
    for turn in range(1, CHIPS + 1):
        peer = lax.rem(chip + turn, CHIPS)

        def mix(step, carry, turn=turn, peer=peer):
            at = pl.ds(pl.multiple_of(step * 24, 24), 24)
            totals = [None] * OUT_LOCAL
            for i in range(BANDS):
                panel = order_ref[i]
                term = window[i, at, :]
                for j in range(OUT_LOCAL):
                    factor = rotations[panel // 2, panel % 2, (peer * 2 + core) * OUT_LOCAL + j]
                    totals[j] = factor * term if i == 0 else totals[j] + factor * term
            for j in range(OUT_LOCAL):
                mixed[turn - 1, j, at, :] = totals[j]
            return carry

        lax.fori_loop(0, CHUNK // 24, mix, 0)
        target = out_ref.at[:, rows(chip), :]
        if turn < CHIPS:
            copy = pltpu.make_async_remote_copy(
                src_ref=mixed.at[turn - 1],
                dst_ref=target,
                send_sem=send_sem.at[1, turn],
                recv_sem=recv_sem.at[1, turn],
                device_id={"band": peer * 2 + core},
                device_id_type=MESH,
            )
        else:
            copy = pltpu.make_async_copy(mixed.at[turn - 1], target, own_sem.at[1])
        copy.start()
        results.append(copy)
    for copy in results:
        copy.wait()


def shards(wave_coeffs, potential, sphere_index, rotation, panel_order):
    f32 = jnp.float32
    values = wave_coeffs.astype(f32).reshape(2, PACKED, 128).transpose(1, 0, 2).reshape(2 * PACKED, 128)
    index = sphere_index.reshape(PACKED, 128)
    inverse_right, inverse_left, inverse_padded = tables(1.0)
    forward_right, forward_left, _ = tables(-1.0)
    grid_shape = jax.ShapeDtypeStruct((GRID_ROWS, 128), f32)
    grid_buffer = pltpu.VMEM((GRID_ROWS, 128), f32)
    dma = pltpu.SemaphoreType.DMA

    def wide(kind):
        return pltpu.VMEM((GUARD + GRID_ROWS, 128), kind)

    real, imag, gap = pl.pallas_call(
        spread_kernel,
        out_shape=(grid_shape, grid_shape, jax.ShapeDtypeStruct((GRID_ROWS, 128), jnp.int32)),
        in_specs=[VMEM_SPEC] * 4,
        out_specs=[VMEM_SPEC] * 3,
        scratch_shapes=[wide(f32), wide(f32), wide(jnp.int32)],
        compiler_params=pltpu.CompilerParams(vmem_limit_bytes=VMEM_BYTES),
        name="spread",
    )(index, values, jnp.asarray(inverse_right), jnp.asarray(inverse_padded))
    real, imag, rotations = pl.pallas_call(
        lines_kernel,
        out_shape=(grid_shape, grid_shape, jax.ShapeDtypeStruct((PARTS, 2, 64), f32)),
        in_specs=[VMEM_SPEC] * 6,
        out_specs=[VMEM_SPEC] * 3,
        scratch_shapes=[grid_buffer] * 4
        + [dma((3, 2, PARTS)), dma((3, 2, PARTS)), dma((3, 2))],
        compiler_params=pltpu.CompilerParams(
            vmem_limit_bytes=VMEM_BYTES, collective_id=0, has_side_effects=True
        ),
        name="lines",
    )(real, imag, potential, rotation, jnp.asarray(inverse_left), jnp.asarray(forward_left))
    plane = pltpu.VMEM((PLANES, NG, 128), f32)
    applied = pl.pallas_call(
        pick_kernel,
        out_shape=jax.ShapeDtypeStruct((2 * PACKED, 128), f32),
        in_specs=[VMEM_SPEC] * 7,
        out_specs=VMEM_SPEC,
        scratch_shapes=[plane, plane, wide(f32), wide(f32), wide(jnp.int32)],
        compiler_params=pltpu.CompilerParams(vmem_limit_bytes=VMEM_BYTES),
        name="pick",
    )(real, imag, gap, values, index, jnp.asarray(forward_left), jnp.asarray(forward_right))
    out = pl.pallas_call(
        rotate_kernel,
        out_shape=jax.ShapeDtypeStruct((OUT_LOCAL, 2 * PACKED, 128), f32),
        in_specs=[VMEM_SPEC, SMEM_SPEC, SMEM_SPEC],
        out_specs=VMEM_SPEC,
        scratch_shapes=[
            pltpu.VMEM((BANDS, CHUNK, 128), f32),
            pltpu.VMEM((CHIPS, OUT_LOCAL, CHUNK, 128), f32),
            dma((2, CHIPS)),
            dma((2, CHIPS)),
            dma((CHIPS,)),
            dma((CHIPS,)),
            dma((2,)),
        ],
        compiler_params=pltpu.CompilerParams(
            vmem_limit_bytes=VMEM_BYTES, collective_id=1, has_side_effects=True
        ),
        name="rotate",
    )(applied, rotations, panel_order)
    return out.reshape(OUT_LOCAL, PACKED, 2, 128).transpose(0, 2, 1, 3).reshape(OUT_LOCAL, 2, PACKED * 128)


def solution(mesh):
    return jax.shard_map(
        shards,
        mesh=mesh,
        in_specs=(P("band", None, "pw"), P(None, "pw"), P("pw"), P("pw", None), P()),
        out_specs=P("band", None, "pw"),
        check_vma=False,
    )
```

```python
import math

import jax
import jax.numpy as jnp
import numpy as np
from jax import lax
from jax.experimental import pallas as pl
from jax.experimental.pallas import tpu as pltpu
from jax.sharding import PartitionSpec as P
import ml_dtypes

NG = 96
PARTS = 8
PLANES = NG // PARTS
GRID_ROWS = PLANES * NG
GROUPS = 3
SENT = 72
GROUP_ROWS = PARTS * SENT
PACKED = 480
CHIPS = 8
CHUNK = 2 * PACKED // CHIPS
PIECES = 3
PIECE = CHUNK // PIECES
BANDS = 16
OUT_LOCAL = 4
GUARD = 512
BLOCK = 96
FLAG = 1 << 20
MESH = pl.DeviceIdType.MESH
VMEM_SPEC = pl.BlockSpec(memory_space=pltpu.VMEM)
SMEM_SPEC = pl.BlockSpec(memory_space=pltpu.SMEM)
HBM_SPEC = pl.BlockSpec(memory_space=pltpu.HBM)
VMEM_BYTES = 48 * 1024 * 1024


def split_table(table):
    high = table.astype(ml_dtypes.bfloat16)
    low = (table - high.astype(np.float64)).astype(ml_dtypes.bfloat16)
    return np.stack([high, low])


def stacked_table(direction, rows, columns):
    row_part, row_at = np.array(rows).T
    column_part, column_at = np.array(columns).T
    angles = 2.0 * math.pi / NG * (np.outer(row_at, column_at) % NG)
    cosines = np.cos(angles) / math.sqrt(NG)
    sines = direction * np.sin(angles) / math.sqrt(NG)
    same = row_part[:, None] == column_part[None, :]
    signs = np.where(row_part == 0, -1.0, 1.0)[:, None]
    return np.where(same, cosines, signs * sines)


def orders():
    natural = [(p, n) for p in range(2) for n in range(NG)]
    sent_y = [(p, PLANES * d + b) for p in range(2) for b in range(PLANES) for d in range(PARTS)]
    got_x = [
        (p, PLANES * s + 4 * g + t)
        for t in range(4) for g in range(GROUPS) for s in range(PARTS) for p in range(2)
    ]
    back_x = [
        (p, PLANES * e + 4 * g + t)
        for t in range(4) for e in range(PARTS) for g in range(GROUPS) for p in range(2)
    ]
    fin_y = [
        (p, PLANES * s + 4 * h + b)
        for p in range(2) for b in range(4) for h in range(GROUPS) for s in range(PARTS)
    ]
    return natural, sent_y, got_x, back_x, fin_y


def left_tables():
    natural, sent_y, got_x, back_x, fin_y = orders()
    return np.stack([
        split_table(stacked_table(1.0, sent_y, natural)),
        split_table(stacked_table(1.0, natural, got_x)),
        split_table(stacked_table(-1.0, back_x, natural)),
        split_table(stacked_table(-1.0, natural, fin_y)),
    ])


def right_tables():
    natural = orders()[0]
    stack = []
    for direction in (1.0, -1.0):
        table = stacked_table(direction, natural, natural).T
        wide = np.zeros((256, 256))
        for p in range(2):
            for q in range(2):
                wide[128 * p : 128 * p + NG, 128 * q : 128 * q + NG] = table[
                    NG * p : NG * p + NG, NG * q : NG * q + NG
                ]
        stack.append(split_table(wide))
    return np.stack(stack)


def split(value):
    high = value.astype(jnp.bfloat16)
    return high, (value - high.astype(jnp.float32)).astype(jnp.bfloat16)


def dot(a, b):
    return jnp.dot(a, b, preferred_element_type=jnp.float32)


def left_transform(table_ref, which, field):
    high, low = split(field)
    return (
        dot(table_ref[which, 0], high) + dot(table_ref[which, 0], low) + dot(table_ref[which, 1], high)
    )


def right_transform(table_ref, which, field):
    high, low = split(field)
    return (
        dot(high, table_ref[which, 0]) + dot(low, table_ref[which, 0]) + dot(high, table_ref[which, 1])
    )


def cell_of(index):
    line = ((index.astype(jnp.float32) + 0.5) * (1.0 / NG)).astype(jnp.int32)
    return line, index - NG * line


def pack_fourth(lane, base, fourth, t):
    return jnp.where(lane < NG, base, pltpu.roll(fourth, NG - 32 * t, 1))


def unpack_fourth(lane, first, second, third):
    return jnp.where(
        lane < 32,
        pltpu.roll(first, 32, 1),
        jnp.where(lane < 64, pltpu.roll(second, 64, 1), pltpu.roll(third, 96, 1)),
    )


def spread_kernel(index_ref, wave_ref, real_ref, imag_ref, leave_ref, vr, vi, gap):
    first_line = lax.axis_index("pw") * GRID_ROWS
    lane = lax.broadcasted_iota(jnp.int32, (BLOCK, 128), 1)
    rows = lax.broadcasted_iota(jnp.int32, (BLOCK, 128), 0)
    gap[...] = jnp.zeros_like(gap)
    for ref in (vr, vi):
        ref[pl.ds(0, GUARD), :] = jnp.zeros((GUARD, 128), jnp.float32)
        ref[pl.ds(GUARD + PACKED, GRID_ROWS - PACKED), :] = jnp.zeros((GRID_ROWS - PACKED, 128), jnp.float32)
    for step in range(PACKED // BLOCK):
        base = step * BLOCK
        line, z = cell_of(index_ref[pl.ds(base, BLOCK), :])
        position = (rows + base) * 128 + lane
        at = pl.ds(GUARD + base, BLOCK)
        gap[at, :] = ((line - first_line) * 128 + z - position) | FLAG
        vr[at, :] = wave_ref[pl.ds(2 * base, BLOCK, stride=2), :]
        vi[at, :] = wave_ref[pl.ds(2 * base + 1, BLOCK, stride=2), :]

    for bit in range(16, -1, -1):
        shift = 1 << bit
        reach = min(PACKED + sum(1 << k for k in range(bit, 17)) // 128 + 1, GRID_ROWS)
        for step in reversed(range(GRID_ROWS // BLOCK)):
            base = step * BLOCK
            leave_at = pl.ds(base, BLOCK)
            if base >= reach:
                if bit == 16:
                    leave_ref[leave_at, :] = jnp.zeros((BLOCK, 128), jnp.int32)
                continue
            here = pl.ds(GUARD + base, BLOCK)
            there = pl.ds(GUARD + base - max(shift // 128, 1), BLOCK)
            own = [ref[here, :] for ref in (gap, vr, vi)]
            other = [ref[there, :] for ref in (gap, vr, vi)]
            if shift < 128:
                stay = lane < 128 - shift
                other = [pltpu.roll(jnp.where(stay, a, b), shift, 1) for a, b in zip(own, other)]
            arrives = (other[0] & shift) != 0
            leaves = own[0] & shift
            left = jnp.where(leaves != 0, 0, own[0])
            held = jnp.where(arrives, other[0], left)
            if bit == 16:
                leave_ref[leave_at, :] = leaves
            else:
                leave_ref[leave_at, :] = leave_ref[leave_at, :] | leaves
            values = [jnp.where(arrives, other[k], own[k]) for k in (1, 2)]
            if bit == 0:
                filled = (held & FLAG) != 0
                real_ref[leave_at, :] = jnp.where(filled, values[0], 0.0)
                imag_ref[leave_at, :] = jnp.where(filled, values[1], 0.0)
            else:
                gap[here, :] = held
                vr[here, :] = values[0]
                vi[here, :] = values[1]


def fields_kernel(
    real_ref, imag_ref, potential_hbm, rotation_ref, left_hbm, right_hbm,
    out_real, out_imag, rotations,
    potential_ref, left_ref, right_ref, send, got, back, fin,
    send_sem, recv_sem, own_sem, small_send, small_recv, load_sem,
):
    me = lax.axis_index("pw")
    peers = [lax.rem(me + turn, PARTS) for turn in range(PARTS)]
    loads = [
        pltpu.make_async_copy(source, target, load_sem.at[k])
        for k, (source, target) in enumerate(
            ((right_hbm, right_ref), (left_hbm, left_ref), (potential_hbm, potential_ref))
        )
    ]
    for load in loads:
        load.start()
    barrier = pltpu.get_barrier_semaphore()
    for peer in peers[1:]:
        pl.semaphore_signal(barrier, inc=1, device_id={"pw": peer}, device_id_type=MESH)

    def start_group(phase, group, source, target):
        copies = []
        for turn, peer in enumerate(peers):
            from_rows = pl.ds(pl.multiple_of(group * GROUP_ROWS + peer * SENT, SENT), SENT)
            to_rows = pl.ds(pl.multiple_of(group * GROUP_ROWS + me * SENT, SENT), SENT)
            if turn:
                copy = pltpu.make_async_remote_copy(
                    src_ref=source.at[from_rows, :],
                    dst_ref=target.at[to_rows, :],
                    send_sem=send_sem.at[phase, group, turn],
                    recv_sem=recv_sem.at[phase, group, turn],
                    device_id={"pw": peer},
                    device_id_type=MESH,
                )
            else:
                copy = pltpu.make_async_copy(
                    source.at[from_rows, :], target.at[to_rows, :], own_sem.at[phase, group]
                )
            copy.start()
            copies.append(copy)
        return copies

    loads[0].wait()
    loads[1].wait()
    lane = lax.broadcasted_iota(jnp.int32, (2 * NG, 128), 1)
    first = []
    for g in range(GROUPS):
        planes = []
        for pair in range(2):
            stacked = []
            for t in (2 * pair, 2 * pair + 1):
                at = pl.ds((4 * g + t) * NG, NG)
                field = jnp.concatenate([real_ref[at, :], imag_ref[at, :]], axis=1).astype(jnp.bfloat16)
                field = dot(field, right_ref[0, 0]) + dot(field, right_ref[0, 1])
                stacked.append(jnp.concatenate([field[:, :128], field[:, 128:]], axis=0))
            both = left_transform(left_ref, 0, jnp.concatenate(stacked, axis=1))
            planes += [both[:, :128], both[:, 128:]]
        for t in range(3):
            packed = pack_fourth(lane, planes[t], planes[3], t)
            for p in range(2):
                for b in range(PLANES):
                    row = (p * PLANES + b) * PARTS
                    at = pl.ds(g * GROUP_ROWS + (p * 3 + t) * PLANES + b, PARTS, stride=SENT)
                    send[at, :] = packed[row : row + PARTS]
        if g == 0:
            pl.semaphore_wait(barrier, PARTS - 1)
        first += start_group(0, g, send, got)

    small = []
    for turn, peer in enumerate(peers):
        if turn:
            copy = pltpu.make_async_remote_copy(
                src_ref=rotation_ref,
                dst_ref=rotations.at[me],
                send_sem=small_send.at[turn],
                recv_sem=small_recv.at[turn],
                device_id={"pw": peer},
                device_id_type=MESH,
            )
        else:
            copy = pltpu.make_async_copy(rotation_ref, rotations.at[me], load_sem.at[3])
        copy.start()
        small.append(copy)

    loads[2].wait()
    for copy in first:
        copy.wait()
    lane48 = lax.broadcasted_iota(jnp.int32, (48, 128), 1)
    second = []
    for group in range(GROUPS):
        for pair in range(2):
            stacked, local = [], []
            for b in (4 * group + 2 * pair, 4 * group + 2 * pair + 1):
                planes = [got[pl.ds(t * PLANES + b, 48, stride=36), :] for t in range(3)]
                planes.append(unpack_fourth(lane48, *planes))
                stacked.append(jnp.concatenate(planes, axis=0))
                offset = b * NG % 128
                start = b * NG - offset
                if offset + NG > 128:
                    part = pltpu.roll(potential_ref[:, start : start + 256], 256 - offset, 1)[:, :128]
                else:
                    part = potential_ref[:, start : start + 128]
                    if offset:
                        part = pltpu.roll(part, 128 - offset, 1)
                local.append(part)
            local = jnp.concatenate(local, axis=1)
            field = left_transform(left_ref, 1, jnp.concatenate(stacked, axis=1))
            field = jnp.concatenate([local, local], axis=0) * field
            field = left_transform(left_ref, 2, field)
            for column in range(2):
                planes = [field[48 * t : 48 * t + 48, 128 * column : 128 * column + 128] for t in range(4)]
                for t in range(3):
                    at = pl.ds(group * GROUP_ROWS + t * 4 + 2 * pair + column, 48, stride=PLANES)
                    back[at, :] = pack_fourth(lane48, planes[t], planes[3], t)
        second += start_group(1, group, back, fin)
    for copy in second + small:
        copy.wait()
    lane96 = lax.broadcasted_iota(jnp.int32, (NG, 128), 1)
    for g in range(GROUPS):
        parts = []
        for p in range(2):
            planes = [
                jnp.concatenate(
                    [
                        fin[pl.ds(g * 24 + p * PLANES + t * 4 + b, 24, stride=SENT), :]
                        for b in range(4)
                    ],
                    axis=0,
                )
                for t in range(3)
            ]
            planes.append(unpack_fourth(lane96, *planes))
            parts.append(planes)
        for pair in range(2):
            stacked = [
                jnp.concatenate([parts[0][t], parts[1][t]], axis=0) for t in (2 * pair, 2 * pair + 1)
            ]
            both = left_transform(left_ref, 3, jnp.concatenate(stacked, axis=1))
            for column in range(2):
                plane = both[:, 128 * column : 128 * column + 128]
                field = jnp.concatenate([plane[:NG], plane[NG:]], axis=1)
                field = right_transform(right_ref, 1, field)
                at = pl.ds((4 * g + 2 * pair + column) * NG, NG)
                out_real[at, :] = field[:, :128]
                out_imag[at, :] = field[:, 128:]


def pick_kernel(back_real, back_imag, leave_ref, wave_ref, index_ref, applied_ref, vr, vi):
    lane = lax.broadcasted_iota(jnp.int32, (BLOCK, 128), 1)
    for ref, source in ((vr, back_real), (vi, back_imag)):
        ref[pl.ds(0, GRID_ROWS), :] = source[...]
        ref[pl.ds(GRID_ROWS, GUARD), :] = jnp.zeros((GUARD, 128), jnp.float32)
    for bit in range(17):
        shift = 1 << bit
        needed = PACKED + sum(1 << k for k in range(bit + 1, 17)) // 128 + 1
        for step in range(GRID_ROWS // BLOCK):
            base = step * BLOCK
            if base >= needed:
                continue
            here = pl.ds(base, BLOCK)
            there = pl.ds(base + max(shift // 128, 1), BLOCK)
            arrives = (leave_ref[here, :] & shift) != 0
            for ref in (vr, vi):
                own, other = ref[here, :], ref[there, :]
                if shift < 128:
                    other = pltpu.roll(jnp.where(lane >= shift, own, other), 128 - shift, 1)
                ref[here, :] = jnp.where(arrives, other, own)

    def signed_square(position):
        signed = jnp.where(position < NG // 2, position, position - NG).astype(jnp.float32)
        return signed * signed

    for step in range(PACKED // BLOCK):
        base = step * BLOCK
        line, z = cell_of(index_ref[pl.ds(base, BLOCK), :])
        x, y = cell_of(line)
        energy = 2.0 * (signed_square(x) + signed_square(y) + signed_square(z)) / float((NG // 2) ** 2)
        for part, ref in enumerate((vr, vi)):
            at = pl.ds(2 * base + part, BLOCK, stride=2)
            applied_ref[at, :] = energy * wave_ref[at, :] + ref[pl.ds(base, BLOCK), :]


def rotate_kernel(
    applied_ref, rotations, order_ref, out_ref,
    window, mixed, send_sem, recv_sem, pair_send, pair_recv, out_send, out_recv, own_sem,
):
    band = lax.axis_index("band")
    chip, core = band // 2, band % 2
    sibling = {"band": chip * 2 + 1 - core}
    peers = [lax.rem(chip + turn, CHIPS) for turn in range(CHIPS)]
    barrier = pltpu.get_barrier_semaphore()
    pl.semaphore_signal(barrier, inc=1, device_id=sibling, device_id_type=MESH)
    for peer in peers[1:]:
        pl.semaphore_signal(barrier, inc=1, device_id={"band": peer * 2 + core}, device_id_type=MESH)
    pl.semaphore_wait(barrier, CHIPS)

    def inner(piece):
        return pl.ds(piece * PIECE, PIECE)

    def outer(which, piece):
        return pl.ds(pl.multiple_of(which * CHUNK + piece * PIECE, PIECE), PIECE)

    sent = []
    for piece in range(PIECES):
        row = []
        for turn, peer in enumerate(peers):
            source = applied_ref.at[outer(peer, piece), :]
            target = window.at[band, inner(piece), :]
            if turn:
                copy = pltpu.make_async_remote_copy(
                    src_ref=source,
                    dst_ref=target,
                    send_sem=send_sem.at[piece, turn],
                    recv_sem=recv_sem.at[piece, turn],
                    device_id={"band": peer * 2 + core},
                    device_id_type=MESH,
                )
            else:
                copy = pltpu.make_async_copy(source, target, own_sem.at[0, piece])
            copy.start()
            row.append(copy)
        sent.append(row)

    pairs, results = [], []
    for piece in range(PIECES):
        row = []
        for turn in range(CHIPS):
            if turn:
                sent[piece][turn].wait_recv()
            else:
                sent[piece][turn].wait()
            source = lax.rem(chip - turn + CHIPS, CHIPS) * 2 + core
            copy = pltpu.make_async_remote_copy(
                src_ref=window.at[source, inner(piece), :],
                dst_ref=window.at[source, inner(piece), :],
                send_sem=pair_send.at[piece, turn],
                recv_sem=pair_recv.at[piece, turn],
                device_id=sibling,
                device_id_type=MESH,
            )
            copy.start()
            row.append(copy)
        for copy in row:
            copy.wait_recv()
        pairs += row
        for turn in range(1, CHIPS + 1):
            peer = peers[turn % CHIPS]
            totals = [None] * OUT_LOCAL
            for i in range(BANDS):
                panel = order_ref[i]
                term = window[i, inner(piece), :]
                for j in range(OUT_LOCAL):
                    factor = rotations[panel // 2, panel % 2, (peer * 2 + core) * OUT_LOCAL + j]
                    totals[j] = factor * term if i == 0 else totals[j] + factor * term
            for j in range(OUT_LOCAL):
                mixed[turn - 1, j, inner(piece), :] = totals[j]
            source = mixed.at[turn - 1, :, inner(piece), :]
            target = out_ref.at[:, outer(chip, piece), :]
            if turn < CHIPS:
                copy = pltpu.make_async_remote_copy(
                    src_ref=source,
                    dst_ref=target,
                    send_sem=out_send.at[piece, turn],
                    recv_sem=out_recv.at[piece, turn],
                    device_id={"band": peer * 2 + core},
                    device_id_type=MESH,
                )
            else:
                copy = pltpu.make_async_copy(source, target, own_sem.at[1, piece])
            copy.start()
            results.append(copy)
    for row in sent:
        for copy in row[1:]:
            copy.wait_send()
    for copy in pairs:
        copy.wait_send()
    for copy in results:
        copy.wait()


def params(**more):
    return pltpu.CompilerParams(vmem_limit_bytes=VMEM_BYTES, **more)


def shards(wave_coeffs, potential, sphere_index, rotation, panel_order):
    f32 = jnp.float32
    bf16 = jnp.bfloat16
    values = wave_coeffs.astype(f32).reshape(2, PACKED, 128).transpose(1, 0, 2).reshape(2 * PACKED, 128)
    index = sphere_index.reshape(PACKED, 128)
    left, right = left_tables(), right_tables()
    grid_shape = jax.ShapeDtypeStruct((GRID_ROWS, 128), f32)
    exchange_buffer = pltpu.VMEM((GROUPS * GROUP_ROWS, 128), f32)
    dma = pltpu.SemaphoreType.DMA

    def wide(kind):
        return pltpu.VMEM((GUARD + GRID_ROWS, 128), kind)

    real, imag, leave = pl.pallas_call(
        spread_kernel,
        out_shape=(grid_shape, grid_shape, jax.ShapeDtypeStruct((GRID_ROWS, 128), jnp.int32)),
        in_specs=[VMEM_SPEC] * 2,
        out_specs=[VMEM_SPEC] * 3,
        scratch_shapes=[wide(f32), wide(f32), wide(jnp.int32)],
        compiler_params=params(),
        name="spread",
    )(index, values)
    real, imag, rotations = pl.pallas_call(
        fields_kernel,
        out_shape=(grid_shape, grid_shape, jax.ShapeDtypeStruct((PARTS, 2, 64), f32)),
        in_specs=[VMEM_SPEC, VMEM_SPEC, HBM_SPEC, VMEM_SPEC, HBM_SPEC, HBM_SPEC],
        out_specs=[VMEM_SPEC] * 3,
        scratch_shapes=[
            pltpu.VMEM(potential.shape, f32),
            pltpu.VMEM(left.shape, bf16),
            pltpu.VMEM(right.shape, bf16),
        ]
        + [exchange_buffer] * 4
        + [dma((2, GROUPS, PARTS)), dma((2, GROUPS, PARTS)), dma((2, GROUPS))]
        + [dma((PARTS,)), dma((PARTS,)), dma((4,))],
        compiler_params=params(collective_id=0, has_side_effects=True),
        name="fields",
    )(real, imag, potential, rotation, jnp.asarray(left), jnp.asarray(right))
    applied = pl.pallas_call(
        pick_kernel,
        out_shape=jax.ShapeDtypeStruct((2 * PACKED, 128), f32),
        in_specs=[VMEM_SPEC] * 5,
        out_specs=VMEM_SPEC,
        scratch_shapes=[wide(f32), wide(f32)],
        compiler_params=params(),
        name="pick",
    )(real, imag, leave, values, index)
    out = pl.pallas_call(
        rotate_kernel,
        out_shape=jax.ShapeDtypeStruct((OUT_LOCAL, 2 * PACKED, 128), f32),
        in_specs=[VMEM_SPEC, SMEM_SPEC, SMEM_SPEC],
        out_specs=VMEM_SPEC,
        scratch_shapes=[
            pltpu.VMEM((BANDS, CHUNK, 128), f32),
            pltpu.VMEM((CHIPS, OUT_LOCAL, CHUNK, 128), f32),
        ]
        + [dma((PIECES, CHIPS))] * 6
        + [dma((2, PIECES))],
        compiler_params=params(collective_id=1, has_side_effects=True),
        name="rotate",
    )(applied, rotations, panel_order)
    return out.reshape(OUT_LOCAL, PACKED, 2, 128).transpose(0, 2, 1, 3).reshape(OUT_LOCAL, 2, PACKED * 128)


def solution(mesh):
    return jax.shard_map(
        shards,
        mesh=mesh,
        in_specs=(P("band", None, "pw"), P(None, "pw"), P("pw"), P("pw", None), P()),
        out_specs=P("band", None, "pw"),
        check_vma=False,
    )
```

```python
import math

import jax
import jax.numpy as jnp
import numpy as np
from jax import lax
from jax.experimental import pallas as pl
from jax.experimental.pallas import tpu as pltpu
from jax.sharding import PartitionSpec as P
import ml_dtypes

NG = 96
PARTS = 8
PLANES = NG // PARTS
GRID_ROWS = PLANES * NG
GROUPS = 3
SENT = 72
GROUP_ROWS = PARTS * SENT
PACKED = 480
CHIPS = 8
CHUNK = 2 * PACKED // CHIPS
PIECES = 3
PIECE = CHUNK // PIECES
BANDS = 16
OUT_LOCAL = 4
GUARD = 512
BLOCK = 96
FLAG = 1 << 20
MESH = pl.DeviceIdType.MESH
VMEM_SPEC = pl.BlockSpec(memory_space=pltpu.VMEM)
SMEM_SPEC = pl.BlockSpec(memory_space=pltpu.SMEM)
HBM_SPEC = pl.BlockSpec(memory_space=pltpu.HBM)
VMEM_BYTES = 60 * 1024 * 1024


def split_table(table):
    high = table.astype(ml_dtypes.bfloat16)
    low = (table - high.astype(np.float64)).astype(ml_dtypes.bfloat16)
    return np.stack([high, low])


def stacked_table(direction, rows, columns):
    row_part, row_at = np.array(rows).T
    column_part, column_at = np.array(columns).T
    angles = 2.0 * math.pi / NG * (np.outer(row_at, column_at) % NG)
    cosines = np.cos(angles) / math.sqrt(NG)
    sines = direction * np.sin(angles) / math.sqrt(NG)
    same = row_part[:, None] == column_part[None, :]
    signs = np.where(row_part == 0, -1.0, 1.0)[:, None]
    return np.where(same, cosines, signs * sines)


def orders():
    natural = [(p, n) for p in range(2) for n in range(NG)]
    sent_y = [(p, PLANES * d + b) for p in range(2) for b in range(PLANES) for d in range(PARTS)]
    got_x = [
        (p, PLANES * s + 4 * g + t)
        for t in range(4) for g in range(GROUPS) for s in range(PARTS) for p in range(2)
    ]
    back_x = [
        (p, PLANES * e + 4 * g + t)
        for t in range(4) for e in range(PARTS) for g in range(GROUPS) for p in range(2)
    ]
    fin_y = [
        (p, PLANES * s + 4 * h + b)
        for p in range(2) for b in range(4) for h in range(GROUPS) for s in range(PARTS)
    ]
    return natural, sent_y, got_x, back_x, fin_y


def left_tables():
    natural, sent_y, got_x, back_x, fin_y = orders()
    return np.stack([
        split_table(stacked_table(1.0, sent_y, natural)),
        split_table(stacked_table(1.0, natural, got_x)),
        split_table(stacked_table(-1.0, back_x, natural)),
        split_table(stacked_table(-1.0, natural, fin_y)),
    ])


def right_tables():
    natural = orders()[0]
    stack = []
    for direction in (1.0, -1.0):
        table = stacked_table(direction, natural, natural).T
        wide = np.zeros((256, 256))
        for p in range(2):
            for q in range(2):
                wide[128 * p : 128 * p + NG, 128 * q : 128 * q + NG] = table[
                    NG * p : NG * p + NG, NG * q : NG * q + NG
                ]
        stack.append(split_table(wide))
    return np.stack(stack)


def split(value):
    high = value.astype(jnp.bfloat16)
    return high, (value - high.astype(jnp.float32)).astype(jnp.bfloat16)


def dot(a, b):
    return jnp.dot(a, b, preferred_element_type=jnp.float32)


def left_transform(table_ref, which, field):
    high, low = split(field)
    return (
        dot(table_ref[which, 0], high) + dot(table_ref[which, 0], low) + dot(table_ref[which, 1], high)
    )


def right_transform(table_ref, which, field):
    high, low = split(field)
    return (
        dot(high, table_ref[which, 0]) + dot(low, table_ref[which, 0]) + dot(high, table_ref[which, 1])
    )


def cell_of(index):
    line = ((index.astype(jnp.float32) + 0.5) * (1.0 / NG)).astype(jnp.int32)
    return line, index - NG * line


def pack_fourth(lane, base, fourth, t):
    return jnp.where(lane < NG, base, pltpu.roll(fourth, NG - 32 * t, 1))


def unpack_fourth(lane, first, second, third):
    return jnp.where(
        lane < 32,
        pltpu.roll(first, 32, 1),
        jnp.where(lane < 64, pltpu.roll(second, 64, 1), pltpu.roll(third, 96, 1)),
    )


def spread(index_ref, wave_ref, real_ref, imag_ref, leave_ref, vr, vi, gap, ready):
    first_line = lax.axis_index("pw") * GRID_ROWS
    lane = lax.broadcasted_iota(jnp.int32, (BLOCK, 128), 1)
    rows = lax.broadcasted_iota(jnp.int32, (BLOCK, 128), 0)
    gap[...] = jnp.zeros_like(gap)
    for ref in (vr, vi):
        ref[pl.ds(0, GUARD), :] = jnp.zeros((GUARD, 128), jnp.float32)
        ref[pl.ds(GUARD + PACKED, GRID_ROWS - PACKED), :] = jnp.zeros((GRID_ROWS - PACKED, 128), jnp.float32)
    ready()
    for step in range(PACKED // BLOCK):
        base = step * BLOCK
        line, z = cell_of(index_ref[pl.ds(base, BLOCK), :])
        position = (rows + base) * 128 + lane
        at = pl.ds(GUARD + base, BLOCK)
        gap[at, :] = ((line - first_line) * 128 + z - position) | FLAG
        vr[at, :] = wave_ref[pl.ds(2 * base, BLOCK, stride=2), :]
        vi[at, :] = wave_ref[pl.ds(2 * base + 1, BLOCK, stride=2), :]

    for bit in range(16, -1, -1):
        shift = 1 << bit
        reach = min(PACKED + sum(1 << k for k in range(bit, 17)) // 128 + 1, GRID_ROWS)
        for step in reversed(range(GRID_ROWS // BLOCK)):
            base = step * BLOCK
            leave_at = pl.ds(base, BLOCK)
            if base >= reach:
                if bit == 16:
                    leave_ref[leave_at, :] = jnp.zeros((BLOCK, 128), jnp.int32)
                continue
            here = pl.ds(GUARD + base, BLOCK)
            there = pl.ds(GUARD + base - max(shift // 128, 1), BLOCK)
            own = [ref[here, :] for ref in (gap, vr, vi)]
            other = [ref[there, :] for ref in (gap, vr, vi)]
            if shift < 128:
                stay = lane < 128 - shift
                other = [pltpu.roll(jnp.where(stay, a, b), shift, 1) for a, b in zip(own, other)]
            arrives = (other[0] & shift) != 0
            leaves = own[0] & shift
            left = jnp.where(leaves != 0, 0, own[0])
            held = jnp.where(arrives, other[0], left)
            if bit == 16:
                leave_ref[leave_at, :] = leaves
            else:
                leave_ref[leave_at, :] = leave_ref[leave_at, :] | leaves
            values = [jnp.where(arrives, other[k], own[k]) for k in (1, 2)]
            if bit == 0:
                filled = (held & FLAG) != 0
                real_ref[leave_at, :] = jnp.where(filled, values[0], 0.0)
                imag_ref[leave_at, :] = jnp.where(filled, values[1], 0.0)
            else:
                gap[here, :] = held
                vr[here, :] = values[0]
                vi[here, :] = values[1]


def fields(
    real_ref, imag_ref, rotation_ref, out_real, out_imag, rotations,
    potential_ref, left_ref, right_ref, send, got, back, fin,
    send_sem, recv_sem, own_sem, small_send, small_recv, small_own, enter, tables_ready, potential_ready,
):
    me = lax.axis_index("pw")
    peers = [lax.rem(me + turn, PARTS) for turn in range(PARTS)]
    def start_group(phase, group, source, target):
        copies = []
        for turn, peer in enumerate(peers):
            from_rows = pl.ds(pl.multiple_of(group * GROUP_ROWS + peer * SENT, SENT), SENT)
            to_rows = pl.ds(pl.multiple_of(group * GROUP_ROWS + me * SENT, SENT), SENT)
            if turn:
                copy = pltpu.make_async_remote_copy(
                    src_ref=source.at[from_rows, :],
                    dst_ref=target.at[to_rows, :],
                    send_sem=send_sem.at[phase, group, turn],
                    recv_sem=recv_sem.at[phase, group, turn],
                    device_id={"pw": peer},
                    device_id_type=MESH,
                )
            else:
                copy = pltpu.make_async_copy(
                    source.at[from_rows, :], target.at[to_rows, :], own_sem.at[phase, group]
                )
            copy.start()
            copies.append(copy)
        return copies

    tables_ready()
    lane = lax.broadcasted_iota(jnp.int32, (2 * NG, 128), 1)
    first = []
    for g in range(GROUPS):
        planes = []
        for pair in range(2):
            stacked = []
            for t in (2 * pair, 2 * pair + 1):
                at = pl.ds((4 * g + t) * NG, NG)
                field = jnp.concatenate([real_ref[at, :], imag_ref[at, :]], axis=1).astype(jnp.bfloat16)
                field = dot(field, right_ref[0, 0]) + dot(field, right_ref[0, 1])
                stacked.append(jnp.concatenate([field[:, :128], field[:, 128:]], axis=0))
            both = left_transform(left_ref, 0, jnp.concatenate(stacked, axis=1))
            planes += [both[:, :128], both[:, 128:]]
        for t in range(3):
            packed = pack_fourth(lane, planes[t], planes[3], t)
            for p in range(2):
                for b in range(PLANES):
                    row = (p * PLANES + b) * PARTS
                    at = pl.ds(g * GROUP_ROWS + (p * 3 + t) * PLANES + b, PARTS, stride=SENT)
                    send[at, :] = packed[row : row + PARTS]
        if g == 0:
            enter()
        first += start_group(0, g, send, got)

    small = []
    for turn, peer in enumerate(peers):
        if turn:
            copy = pltpu.make_async_remote_copy(
                src_ref=rotation_ref,
                dst_ref=rotations.at[me],
                send_sem=small_send.at[turn],
                recv_sem=small_recv.at[turn],
                device_id={"pw": peer},
                device_id_type=MESH,
            )
        else:
            copy = pltpu.make_async_copy(rotation_ref, rotations.at[me], small_own.at[0])
        copy.start()
        small.append(copy)

    potential_ready()
    for copy in first:
        copy.wait()
    lane48 = lax.broadcasted_iota(jnp.int32, (48, 128), 1)
    second = []
    for group in range(GROUPS):
        for pair in range(2):
            stacked, local = [], []
            for b in (4 * group + 2 * pair, 4 * group + 2 * pair + 1):
                planes = [got[pl.ds(t * PLANES + b, 48, stride=36), :] for t in range(3)]
                planes.append(unpack_fourth(lane48, *planes))
                stacked.append(jnp.concatenate(planes, axis=0))
                offset = b * NG % 128
                start = b * NG - offset
                if offset + NG > 128:
                    part = pltpu.roll(potential_ref[:, start : start + 256], 256 - offset, 1)[:, :128]
                else:
                    part = potential_ref[:, start : start + 128]
                    if offset:
                        part = pltpu.roll(part, 128 - offset, 1)
                local.append(part)
            local = jnp.concatenate(local, axis=1)
            field = left_transform(left_ref, 1, jnp.concatenate(stacked, axis=1))
            field = jnp.concatenate([local, local], axis=0) * field
            field = left_transform(left_ref, 2, field)
            for column in range(2):
                planes = [field[48 * t : 48 * t + 48, 128 * column : 128 * column + 128] for t in range(4)]
                for t in range(3):
                    at = pl.ds(group * GROUP_ROWS + t * 4 + 2 * pair + column, 48, stride=PLANES)
                    back[at, :] = pack_fourth(lane48, planes[t], planes[3], t)
        second += start_group(1, group, back, fin)
    for copy in second + small:
        copy.wait()
    lane96 = lax.broadcasted_iota(jnp.int32, (NG, 128), 1)
    for g in range(GROUPS):
        parts = []
        for p in range(2):
            planes = [
                jnp.concatenate(
                    [
                        fin[pl.ds(g * 24 + p * PLANES + t * 4 + b, 24, stride=SENT), :]
                        for b in range(4)
                    ],
                    axis=0,
                )
                for t in range(3)
            ]
            planes.append(unpack_fourth(lane96, *planes))
            parts.append(planes)
        for pair in range(2):
            stacked = [
                jnp.concatenate([parts[0][t], parts[1][t]], axis=0) for t in (2 * pair, 2 * pair + 1)
            ]
            both = left_transform(left_ref, 3, jnp.concatenate(stacked, axis=1))
            for column in range(2):
                plane = both[:, 128 * column : 128 * column + 128]
                field = jnp.concatenate([plane[:NG], plane[NG:]], axis=1)
                field = right_transform(right_ref, 1, field)
                at = pl.ds((4 * g + 2 * pair + column) * NG, NG)
                out_real[at, :] = field[:, :128]
                out_imag[at, :] = field[:, 128:]


def pick(leave_ref, wave_ref, index_ref, applied_ref, vr, vi):
    lane = lax.broadcasted_iota(jnp.int32, (BLOCK, 128), 1)
    for bit in range(17):
        shift = 1 << bit
        needed = PACKED + sum(1 << k for k in range(bit + 1, 17)) // 128 + 1
        for step in range(GRID_ROWS // BLOCK):
            base = step * BLOCK
            if base >= needed:
                continue
            here = pl.ds(base, BLOCK)
            there = pl.ds(base + max(shift // 128, 1), BLOCK)
            arrives = (leave_ref[here, :] & shift) != 0
            for ref in (vr, vi):
                own, other = ref[here, :], ref[there, :]
                if shift < 128:
                    other = pltpu.roll(jnp.where(lane >= shift, own, other), 128 - shift, 1)
                ref[here, :] = jnp.where(arrives, other, own)

    def signed_square(position):
        signed = jnp.where(position < NG // 2, position, position - NG).astype(jnp.float32)
        return signed * signed

    for step in range(PACKED // BLOCK):
        base = step * BLOCK
        line, z = cell_of(index_ref[pl.ds(base, BLOCK), :])
        x, y = cell_of(line)
        energy = 2.0 * (signed_square(x) + signed_square(y) + signed_square(z)) / float((NG // 2) ** 2)
        for part, ref in enumerate((vr, vi)):
            at = pl.ds(2 * base + part, BLOCK, stride=2)
            applied_ref[at, :] = energy * wave_ref[at, :] + ref[pl.ds(base, BLOCK), :]


def rotate(
    applied_ref, rotations, order_ref, out_ref,
    window, mixed, send_sem, recv_sem, pair_send, pair_recv, out_send, out_recv, own_sem,
):
    band = lax.axis_index("band")
    chip, core = band // 2, band % 2
    sibling = {"band": chip * 2 + 1 - core}
    peers = [lax.rem(chip + turn, CHIPS) for turn in range(CHIPS)]
    def inner(piece):
        return pl.ds(piece * PIECE, PIECE)

    def outer(which, piece):
        return pl.ds(pl.multiple_of(which * CHUNK + piece * PIECE, PIECE), PIECE)

    sent = []
    for piece in range(PIECES):
        row = []
        for turn, peer in enumerate(peers):
            source = applied_ref.at[outer(peer, piece), :]
            target = window.at[band, inner(piece), :]
            if turn:
                copy = pltpu.make_async_remote_copy(
                    src_ref=source,
                    dst_ref=target,
                    send_sem=send_sem.at[piece, turn],
                    recv_sem=recv_sem.at[piece, turn],
                    device_id={"band": peer * 2 + core},
                    device_id_type=MESH,
                )
            else:
                copy = pltpu.make_async_copy(source, target, own_sem.at[0, piece])
            copy.start()
            row.append(copy)
        sent.append(row)

    pairs, results = [], []
    for piece in range(PIECES):
        row = []
        for turn in range(CHIPS):
            if turn:
                sent[piece][turn].wait_recv()
            else:
                sent[piece][turn].wait()
            source = lax.rem(chip - turn + CHIPS, CHIPS) * 2 + core
            copy = pltpu.make_async_remote_copy(
                src_ref=window.at[source, inner(piece), :],
                dst_ref=window.at[source, inner(piece), :],
                send_sem=pair_send.at[piece, turn],
                recv_sem=pair_recv.at[piece, turn],
                device_id=sibling,
                device_id_type=MESH,
            )
            copy.start()
            row.append(copy)
        for copy in row:
            copy.wait_recv()
        pairs += row
        for turn in range(1, CHIPS + 1):
            peer = peers[turn % CHIPS]
            totals = [None] * OUT_LOCAL
            for i in range(BANDS):
                panel = order_ref[i]
                term = window[i, inner(piece), :]
                for j in range(OUT_LOCAL):
                    factor = rotations[panel // 2, panel % 2, (peer * 2 + core) * OUT_LOCAL + j]
                    totals[j] = factor * term if i == 0 else totals[j] + factor * term
            for j in range(OUT_LOCAL):
                mixed[turn - 1, j, inner(piece), :] = totals[j]
            source = mixed.at[turn - 1, :, inner(piece), :]
            target = out_ref.at[:, outer(chip, piece), :]
            if turn < CHIPS:
                copy = pltpu.make_async_remote_copy(
                    src_ref=source,
                    dst_ref=target,
                    send_sem=out_send.at[piece, turn],
                    recv_sem=out_recv.at[piece, turn],
                    device_id={"band": peer * 2 + core},
                    device_id_type=MESH,
                )
            else:
                copy = pltpu.make_async_copy(source, target, own_sem.at[1, piece])
            copy.start()
            results.append(copy)
    for row in sent:
        for copy in row[1:]:
            copy.wait_send()
    for copy in pairs:
        copy.wait_send()
    for copy in results:
        copy.wait()


def whole_kernel(
    index_hbm, wave_hbm, potential_hbm, rotation_ref, order_ref, left_hbm, right_hbm,
    out_ref,
    index_ref, wave_ref, potential_ref, left_ref, right_ref,
    real_ref, imag_ref, leave_ref, vr, vi, gap, send, got, back, fin, rotations, factors, applied_ref, window, mixed,
    load_sem, send_sem, recv_sem, own_sem, small_send, small_recv, small_own,
    first_send, first_recv, pair_send, pair_recv, out_send, out_recv, band_own,
):
    loads = [
        pltpu.make_async_copy(source, target, load_sem.at[k])
        for k, (source, target) in enumerate((
            (index_hbm, index_ref), (wave_hbm, wave_ref), (right_hbm, right_ref),
            (left_hbm, left_ref), (potential_hbm, potential_ref),
        ))
    ]
    for load in loads:
        load.start()
    me, band = lax.axis_index("pw"), lax.axis_index("band")
    chip, core = band // 2, band % 2
    barrier = pltpu.get_barrier_semaphore()
    for turn in range(1, PARTS):
        pl.semaphore_signal(
            barrier, inc=1, device_id={"pw": lax.rem(me + turn, PARTS)}, device_id_type=MESH
        )
    for turn in range(1, CHIPS):
        peer = lax.rem(chip + turn, CHIPS) * 2 + core
        pl.semaphore_signal(barrier, inc=1, device_id={"band": peer}, device_id_type=MESH)
    pl.semaphore_signal(barrier, inc=1, device_id={"band": chip * 2 + 1 - core}, device_id_type=MESH)

    def ready(*which):
        def wait():
            for k in which:
                loads[k].wait()

        return wait

    spread(index_ref, wave_ref, real_ref, imag_ref, leave_ref, vr, vi, gap, ready(0, 1))
    fields(
        real_ref, imag_ref, rotation_ref, vr, vi, rotations,
        potential_ref, left_ref, right_ref, send, got, back, fin,
        send_sem, recv_sem, own_sem, small_send, small_recv, small_own,
        lambda: pl.semaphore_wait(barrier, PARTS - 1 + CHIPS), ready(2, 3), ready(4),
    )
    to_scalars = pltpu.make_async_copy(rotations, factors, small_own.at[1])
    to_scalars.start()
    pick(leave_ref, wave_ref, index_ref, applied_ref, vr, vi)
    to_scalars.wait()
    rotate(
        applied_ref, factors, order_ref, out_ref, window, mixed,
        first_send, first_recv, pair_send, pair_recv, out_send, out_recv, band_own,
    )


def shards(wave_coeffs, potential, sphere_index, rotation, panel_order):
    f32 = jnp.float32
    bf16 = jnp.bfloat16
    values = wave_coeffs.astype(f32).reshape(2, PACKED, 128).transpose(1, 0, 2).reshape(2 * PACKED, 128)
    index = sphere_index.reshape(PACKED, 128)
    left, right = left_tables(), right_tables()
    exchange_buffer = pltpu.VMEM((GROUPS * GROUP_ROWS, 128), f32)
    grid_buffer = pltpu.VMEM((GRID_ROWS, 128), f32)
    dma = pltpu.SemaphoreType.DMA

    def wide(kind):
        return pltpu.VMEM((GUARD + GRID_ROWS, 128), kind)

    out = pl.pallas_call(
        whole_kernel,
        out_shape=jax.ShapeDtypeStruct((OUT_LOCAL, 2 * PACKED, 128), f32),
        in_specs=[HBM_SPEC, HBM_SPEC, HBM_SPEC, VMEM_SPEC, SMEM_SPEC, HBM_SPEC, HBM_SPEC],
        out_specs=HBM_SPEC,
        scratch_shapes=[
            pltpu.VMEM((PACKED, 128), jnp.int32),
            pltpu.VMEM((2 * PACKED, 128), f32),
            pltpu.VMEM(potential.shape, f32),
            pltpu.VMEM(left.shape, bf16),
            pltpu.VMEM(right.shape, bf16),
            grid_buffer,
            grid_buffer,
            pltpu.VMEM((GRID_ROWS, 128), jnp.int32),
            wide(f32),
            wide(f32),
            wide(jnp.int32),
        ]
        + [exchange_buffer] * 4
        + [
            pltpu.VMEM((PARTS, 2, 64), f32),
            pltpu.SMEM((PARTS, 2, 64), f32),
            pltpu.VMEM((2 * PACKED, 128), f32),
            pltpu.VMEM((BANDS, CHUNK, 128), f32),
            pltpu.VMEM((CHIPS, OUT_LOCAL, CHUNK, 128), f32),
            dma((5,)),
            dma((2, GROUPS, PARTS)),
            dma((2, GROUPS, PARTS)),
            dma((2, GROUPS)),
            dma((PARTS,)),
            dma((PARTS,)),
            dma((2,)),
        ]
        + [dma((PIECES, CHIPS))] * 6
        + [dma((2, PIECES))],
        compiler_params=pltpu.CompilerParams(
            vmem_limit_bytes=VMEM_BYTES, collective_id=0, has_side_effects=True
        ),
        name="whole",
    )(index, values, potential, rotation, panel_order, jnp.asarray(left), jnp.asarray(right))
    return out.reshape(OUT_LOCAL, PACKED, 2, 128).transpose(0, 2, 1, 3).reshape(OUT_LOCAL, 2, PACKED * 128)


def solution(mesh):
    return jax.shard_map(
        shards,
        mesh=mesh,
        in_specs=(P("band", None, "pw"), P(None, "pw"), P("pw"), P("pw", None), P()),
        out_specs=P("band", None, "pw"),
        check_vma=False,
    )
```

```python
import math

import jax
import jax.numpy as jnp
import numpy as np
from jax import lax
from jax.experimental import pallas as pl
from jax.experimental.pallas import tpu as pltpu
from jax.sharding import PartitionSpec as P
import ml_dtypes

NG = 96
PARTS = 8
PLANES = NG // PARTS
GRID_ROWS = PLANES * NG
GROUPS = 3
SENT = 72
GROUP_ROWS = PARTS * SENT
PACKED = 480
CHIPS = 8
CUBE = ((4, (0, 1, 3, 2)), (1, (0, 3, 4, 7)), (3, (0, 1, 4, 5)))
PIECES = len(CUBE)
PARTED = 4
CHUNK = 2 * PACKED // PIECES // PARTED
HALF = CHUNK // 2
BANDS = 16
OUT_LOCAL = 4
GUARD = 512
BLOCK = 96
FLAG = 1 << 20
MESH = pl.DeviceIdType.MESH
VMEM_SPEC = pl.BlockSpec(memory_space=pltpu.VMEM)
SMEM_SPEC = pl.BlockSpec(memory_space=pltpu.SMEM)
HBM_SPEC = pl.BlockSpec(memory_space=pltpu.HBM)
VMEM_BYTES = 60 * 1024 * 1024


def split_table(table):
    high = table.astype(ml_dtypes.bfloat16)
    low = (table - high.astype(np.float64)).astype(ml_dtypes.bfloat16)
    return np.stack([high, low])


def stacked_table(direction, rows, columns):
    row_part, row_at = np.array(rows).T
    column_part, column_at = np.array(columns).T
    angles = 2.0 * math.pi / NG * (np.outer(row_at, column_at) % NG)
    cosines = np.cos(angles) / math.sqrt(NG)
    sines = direction * np.sin(angles) / math.sqrt(NG)
    same = row_part[:, None] == column_part[None, :]
    signs = np.where(row_part == 0, -1.0, 1.0)[:, None]
    return np.where(same, cosines, signs * sines)


def orders():
    natural = [(p, n) for p in range(2) for n in range(NG)]
    sent_y = [(p, PLANES * d + b) for p in range(2) for b in range(PLANES) for d in range(PARTS)]
    got_x = [
        (p, PLANES * s + 4 * g + t)
        for t in range(4) for g in range(GROUPS) for s in range(PARTS) for p in range(2)
    ]
    back_x = [
        (p, PLANES * e + 4 * g + t)
        for t in range(4) for e in range(PARTS) for g in range(GROUPS) for p in range(2)
    ]
    fin_y = [
        (p, PLANES * s + 4 * h + b)
        for p in range(2) for b in range(4) for h in range(GROUPS) for s in range(PARTS)
    ]
    return natural, sent_y, got_x, back_x, fin_y


def left_tables():
    natural, sent_y, got_x, back_x, fin_y = orders()
    return np.stack([
        split_table(stacked_table(1.0, sent_y, natural)),
        split_table(stacked_table(1.0, natural, got_x)),
        split_table(stacked_table(-1.0, back_x, natural)),
        split_table(stacked_table(-1.0, natural, fin_y)),
    ])


def right_tables():
    natural = orders()[0]
    stack = []
    for direction in (1.0, -1.0):
        table = stacked_table(direction, natural, natural).T
        wide = np.zeros((256, 256))
        for p in range(2):
            for q in range(2):
                wide[128 * p : 128 * p + NG, 128 * q : 128 * q + NG] = table[
                    NG * p : NG * p + NG, NG * q : NG * q + NG
                ]
        stack.append(split_table(wide))
    return np.stack(stack)


def split(value):
    high = value.astype(jnp.bfloat16)
    return high, (value - high.astype(jnp.float32)).astype(jnp.bfloat16)


def dot(a, b):
    return jnp.dot(a, b, preferred_element_type=jnp.float32)


def left_transform(table_ref, which, field):
    high, low = split(field)
    return (
        dot(table_ref[which, 0], high) + dot(table_ref[which, 0], low) + dot(table_ref[which, 1], high)
    )


def right_transform(table_ref, which, field):
    high, low = split(field)
    return (
        dot(high, table_ref[which, 0]) + dot(low, table_ref[which, 0]) + dot(high, table_ref[which, 1])
    )


def cell_of(index):
    line = ((index.astype(jnp.float32) + 0.5) * (1.0 / NG)).astype(jnp.int32)
    return line, index - NG * line


def pack_fourth(lane, base, fourth, t):
    return jnp.where(lane < NG, base, pltpu.roll(fourth, NG - 32 * t, 1))


def unpack_fourth(lane, first, second, third):
    return jnp.where(
        lane < 32,
        pltpu.roll(first, 32, 1),
        jnp.where(lane < 64, pltpu.roll(second, 64, 1), pltpu.roll(third, 96, 1)),
    )


def spread(index_ref, wave_ref, real_ref, imag_ref, leave_ref, vr, vi, gap, ready):
    first_line = lax.axis_index("pw") * GRID_ROWS
    lane = lax.broadcasted_iota(jnp.int32, (BLOCK, 128), 1)
    rows = lax.broadcasted_iota(jnp.int32, (BLOCK, 128), 0)
    gap[...] = jnp.zeros_like(gap)
    for ref in (vr, vi):
        ref[pl.ds(0, GUARD), :] = jnp.zeros((GUARD, 128), jnp.float32)
        ref[pl.ds(GUARD + PACKED, GRID_ROWS - PACKED), :] = jnp.zeros((GRID_ROWS - PACKED, 128), jnp.float32)
    ready()
    for step in range(PACKED // BLOCK):
        base = step * BLOCK
        line, z = cell_of(index_ref[pl.ds(base, BLOCK), :])
        position = (rows + base) * 128 + lane
        at = pl.ds(GUARD + base, BLOCK)
        gap[at, :] = ((line - first_line) * 128 + z - position) | FLAG
        vr[at, :] = wave_ref[pl.ds(2 * base, BLOCK, stride=2), :]
        vi[at, :] = wave_ref[pl.ds(2 * base + 1, BLOCK, stride=2), :]

    for bit in range(16, -1, -1):
        shift = 1 << bit
        reach = min(PACKED + sum(1 << k for k in range(bit, 17)) // 128 + 1, GRID_ROWS)
        for step in reversed(range(GRID_ROWS // BLOCK)):
            base = step * BLOCK
            leave_at = pl.ds(base, BLOCK)
            if base >= reach:
                if bit == 16:
                    leave_ref[leave_at, :] = jnp.zeros((BLOCK, 128), jnp.int32)
                continue
            here = pl.ds(GUARD + base, BLOCK)
            there = pl.ds(GUARD + base - max(shift // 128, 1), BLOCK)
            own = [ref[here, :] for ref in (gap, vr, vi)]
            other = [ref[there, :] for ref in (gap, vr, vi)]
            if shift < 128:
                stay = lane < 128 - shift
                other = [pltpu.roll(jnp.where(stay, a, b), shift, 1) for a, b in zip(own, other)]
            arrives = (other[0] & shift) != 0
            leaves = own[0] & shift
            left = jnp.where(leaves != 0, 0, own[0])
            held = jnp.where(arrives, other[0], left)
            if bit == 16:
                leave_ref[leave_at, :] = leaves
            else:
                leave_ref[leave_at, :] = leave_ref[leave_at, :] | leaves
            values = [jnp.where(arrives, other[k], own[k]) for k in (1, 2)]
            if bit == 0:
                filled = (held & FLAG) != 0
                real_ref[leave_at, :] = jnp.where(filled, values[0], 0.0)
                imag_ref[leave_at, :] = jnp.where(filled, values[1], 0.0)
            else:
                gap[here, :] = held
                vr[here, :] = values[0]
                vi[here, :] = values[1]


def fields(
    real_ref, imag_ref, rotation_ref, out_real, out_imag, rotations,
    potential_ref, left_ref, right_ref, send, got, back, fin,
    send_sem, recv_sem, own_sem, small_send, small_recv, small_own, enter, tables_ready, potential_ready,
):
    me = lax.axis_index("pw")
    peers = [lax.rem(me + turn, PARTS) for turn in range(PARTS)]
    def start_group(phase, group, source, target):
        copies = []
        for turn, peer in enumerate(peers):
            from_rows = pl.ds(pl.multiple_of(group * GROUP_ROWS + peer * SENT, SENT), SENT)
            to_rows = pl.ds(pl.multiple_of(group * GROUP_ROWS + me * SENT, SENT), SENT)
            if turn:
                copy = pltpu.make_async_remote_copy(
                    src_ref=source.at[from_rows, :],
                    dst_ref=target.at[to_rows, :],
                    send_sem=send_sem.at[phase, group, turn],
                    recv_sem=recv_sem.at[phase, group, turn],
                    device_id={"pw": peer},
                    device_id_type=MESH,
                )
            else:
                copy = pltpu.make_async_copy(
                    source.at[from_rows, :], target.at[to_rows, :], own_sem.at[phase, group]
                )
            copy.start()
            copies.append(copy)
        return copies

    tables_ready()
    lane = lax.broadcasted_iota(jnp.int32, (2 * NG, 128), 1)
    first = []
    for g in range(GROUPS):
        planes = []
        for pair in range(2):
            stacked = []
            for t in (2 * pair, 2 * pair + 1):
                at = pl.ds((4 * g + t) * NG, NG)
                field = jnp.concatenate([real_ref[at, :], imag_ref[at, :]], axis=1).astype(jnp.bfloat16)
                field = dot(field, right_ref[0, 0]) + dot(field, right_ref[0, 1])
                stacked.append(jnp.concatenate([field[:, :128], field[:, 128:]], axis=0))
            both = left_transform(left_ref, 0, jnp.concatenate(stacked, axis=1))
            planes += [both[:, :128], both[:, 128:]]
        for t in range(3):
            packed = pack_fourth(lane, planes[t], planes[3], t)
            for p in range(2):
                for b in range(PLANES):
                    row = (p * PLANES + b) * PARTS
                    at = pl.ds(g * GROUP_ROWS + (p * 3 + t) * PLANES + b, PARTS, stride=SENT)
                    send[at, :] = packed[row : row + PARTS]
        if g == 0:
            enter()
        first += start_group(0, g, send, got)

    small = []
    for turn, peer in enumerate(peers):
        if turn:
            copy = pltpu.make_async_remote_copy(
                src_ref=rotation_ref,
                dst_ref=rotations.at[me],
                send_sem=small_send.at[turn],
                recv_sem=small_recv.at[turn],
                device_id={"pw": peer},
                device_id_type=MESH,
            )
        else:
            copy = pltpu.make_async_copy(rotation_ref, rotations.at[me], small_own.at[0])
        copy.start()
        small.append(copy)

    potential_ready()
    for copy in first:
        copy.wait()
    lane48 = lax.broadcasted_iota(jnp.int32, (48, 128), 1)
    second = []
    for group in range(GROUPS):
        for pair in range(2):
            stacked, local = [], []
            for b in (4 * group + 2 * pair, 4 * group + 2 * pair + 1):
                planes = [got[pl.ds(t * PLANES + b, 48, stride=36), :] for t in range(3)]
                planes.append(unpack_fourth(lane48, *planes))
                stacked.append(jnp.concatenate(planes, axis=0))
                offset = b * NG % 128
                start = b * NG - offset
                if offset + NG > 128:
                    part = pltpu.roll(potential_ref[:, start : start + 256], 256 - offset, 1)[:, :128]
                else:
                    part = potential_ref[:, start : start + 128]
                    if offset:
                        part = pltpu.roll(part, 128 - offset, 1)
                local.append(part)
            local = jnp.concatenate(local, axis=1)
            field = left_transform(left_ref, 1, jnp.concatenate(stacked, axis=1))
            field = jnp.concatenate([local, local], axis=0) * field
            field = left_transform(left_ref, 2, field)
            for column in range(2):
                planes = [field[48 * t : 48 * t + 48, 128 * column : 128 * column + 128] for t in range(4)]
                for t in range(3):
                    at = pl.ds(group * GROUP_ROWS + t * 4 + 2 * pair + column, 48, stride=PLANES)
                    back[at, :] = pack_fourth(lane48, planes[t], planes[3], t)
        second += start_group(1, group, back, fin)
    for copy in second + small:
        copy.wait()
    lane96 = lax.broadcasted_iota(jnp.int32, (NG, 128), 1)
    for g in range(GROUPS):
        parts = []
        for p in range(2):
            planes = [
                jnp.concatenate(
                    [
                        fin[pl.ds(g * 24 + p * PLANES + t * 4 + b, 24, stride=SENT), :]
                        for b in range(4)
                    ],
                    axis=0,
                )
                for t in range(3)
            ]
            planes.append(unpack_fourth(lane96, *planes))
            parts.append(planes)
        for pair in range(2):
            stacked = [
                jnp.concatenate([parts[0][t], parts[1][t]], axis=0) for t in (2 * pair, 2 * pair + 1)
            ]
            both = left_transform(left_ref, 3, jnp.concatenate(stacked, axis=1))
            for column in range(2):
                plane = both[:, 128 * column : 128 * column + 128]
                field = jnp.concatenate([plane[:NG], plane[NG:]], axis=1)
                field = right_transform(right_ref, 1, field)
                at = pl.ds((4 * g + 2 * pair + column) * NG, NG)
                out_real[at, :] = field[:, :128]
                out_imag[at, :] = field[:, 128:]


def pick(leave_ref, wave_ref, index_ref, applied_ref, vr, vi):
    lane = lax.broadcasted_iota(jnp.int32, (BLOCK, 128), 1)
    for bit in range(17):
        shift = 1 << bit
        needed = PACKED + sum(1 << k for k in range(bit + 1, 17)) // 128 + 1
        for step in range(GRID_ROWS // BLOCK):
            base = step * BLOCK
            if base >= needed:
                continue
            here = pl.ds(base, BLOCK)
            there = pl.ds(base + max(shift // 128, 1), BLOCK)
            arrives = (leave_ref[here, :] & shift) != 0
            for ref in (vr, vi):
                own, other = ref[here, :], ref[there, :]
                if shift < 128:
                    other = pltpu.roll(jnp.where(lane >= shift, own, other), 128 - shift, 1)
                ref[here, :] = jnp.where(arrives, other, own)

    def signed_square(position):
        signed = jnp.where(position < NG // 2, position, position - NG).astype(jnp.float32)
        return signed * signed

    for step in range(PACKED // BLOCK):
        base = step * BLOCK
        line, z = cell_of(index_ref[pl.ds(base, BLOCK), :])
        x, y = cell_of(line)
        energy = 2.0 * (signed_square(x) + signed_square(y) + signed_square(z)) / float((NG // 2) ** 2)
        for part, ref in enumerate((vr, vi)):
            at = pl.ds(2 * base + part, BLOCK, stride=2)
            applied_ref[at, :] = energy * wave_ref[at, :] + ref[pl.ds(base, BLOCK), :]


def across(chip, mask):
    z, x = chip // 4, chip % 4
    x = (x, x + 1 - 2 * (x % 2), (x + 2) % 4, 3 - x)[mask % 4]
    return (1 - z if mask >= 4 else z) * 4 + x


def part_of(chip, piece):
    z, x = chip // 4, chip % 4
    near, far = (x + x // 2) % 2, x // 2
    return (near + 2 * far, far + 2 * z, near + 2 * z)[piece]


def rotate(
    applied_ref, rotations, order_ref, out_ref, window, mixed,
    first_send, first_recv, relay_send, relay_recv, out_send, out_recv, own_sem,
):
    band = lax.axis_index("band")
    chip, core = band // 2, band % 2
    cores = (core, 1 - core)

    def rows(which, piece, half):
        start = piece * PARTED * CHUNK + part_of(which, piece) * CHUNK + half * HALF
        return pl.ds(pl.multiple_of(start, HALF), HALF)

    def move(source, target, peer, turn, send, recv, own):
        if turn:
            copy = pltpu.make_async_remote_copy(
                src_ref=source,
                dst_ref=target,
                send_sem=send,
                recv_sem=recv,
                device_id={"band": peer},
                device_id_type=MESH,
            )
        else:
            copy = pltpu.make_async_copy(source, target, own)
        copy.start()
        return copy

    sent, relayed, results = [], [], []
    for piece, (_, masks) in enumerate(CUBE):
        copies = []
        for k, mask in enumerate(masks):
            peer = across(chip, mask)
            for c, half in enumerate(cores):
                turn = 2 * k + c
                copies.append(move(
                    applied_ref.at[rows(peer, piece, half), :], window.at[piece, 2 * k + core],
                    peer * 2 + half, turn, first_send.at[piece, turn], first_recv.at[piece, turn],
                    own_sem.at[0, piece],
                ))
        sent.append(copies)

    def relay(piece):
        sent[piece][0].wait()
        for copy in sent[piece][1:]:
            copy.wait_recv()
        relayed.append(move(
            window.at[piece, pl.ds(0, CHIPS)], window.at[piece, pl.ds(CHIPS, CHIPS)],
            across(chip, CUBE[piece][0]) * 2 + core, 1, relay_send.at[piece], relay_recv.at[piece], None,
        ))

    def mix(piece):
        shared, masks = CUBE[piece]
        relayed[piece].wait_recv()
        panels = []
        for start in (chip, across(chip, shared)):
            for mask in masks:
                for c in range(2):
                    panel = order_ref[across(start, mask) * 2 + c]
                    panels.append((panel // 2, panel % 2))
        for k in reversed(range(len(masks))):
            for c in (1, 0):
                peer = across(chip, masks[k]) * 2 + cores[c]
                turn = 2 * k + c
                totals = [None] * OUT_LOCAL
                for i in range(BANDS):
                    term = window[piece, i]
                    for j in range(OUT_LOCAL):
                        factor = rotations[panels[i][0], panels[i][1], peer * OUT_LOCAL + j]
                        totals[j] = factor * term if i == 0 else totals[j] + factor * term
                for j in range(OUT_LOCAL):
                    mixed[piece, turn, j] = totals[j]
                results.append(move(
                    mixed.at[piece, turn], out_ref.at[:, rows(chip, piece, core), :],
                    peer, turn, out_send.at[piece, turn], out_recv.at[piece, turn], own_sem.at[1, piece],
                ))

    for piece in range(PIECES):
        relay(piece)
    for piece in range(PIECES):
        mix(piece)
    for copies in sent:
        for copy in copies[1:]:
            copy.wait_send()
    for copy in relayed:
        copy.wait_send()
    for copy in results:
        copy.wait()


def whole_kernel(
    index_hbm, wave_hbm, potential_hbm, rotation_ref, order_ref, left_hbm, right_hbm,
    out_ref,
    index_ref, narrow_ref, wave_ref, potential_ref, left_ref, right_ref,
    real_ref, imag_ref, leave_ref, vr, vi, gap, send, got, back, fin, rotations, factors, applied_ref, window, mixed,
    load_sem, send_sem, recv_sem, own_sem, small_send, small_recv, small_own,
    first_send, first_recv, relay_send, relay_recv, out_send, out_recv, band_own,
):
    loads = [
        pltpu.make_async_copy(source, target, load_sem.at[k])
        for k, (source, target) in enumerate((
            (index_hbm, index_ref), (wave_hbm, narrow_ref), (right_hbm, right_ref),
            (left_hbm, left_ref), (potential_hbm, potential_ref),
        ))
    ]
    for load in loads:
        load.start()
    me, band = lax.axis_index("pw"), lax.axis_index("band")
    barrier = pltpu.get_barrier_semaphore()
    for turn in range(1, PARTS):
        pl.semaphore_signal(
            barrier, inc=1, device_id={"pw": lax.rem(me + turn, PARTS)}, device_id_type=MESH
        )
    for turn in range(1, BANDS):
        peer = lax.rem(band + turn, BANDS)
        pl.semaphore_signal(barrier, inc=1, device_id={"band": peer}, device_id_type=MESH)

    def ready(*which):
        def wait():
            for k in which:
                loads[k].wait()

        return wait

    def inputs_ready():
        ready(0, 1)()
        wave_ref[...] = narrow_ref[...].astype(jnp.float32)

    spread(index_ref, wave_ref, real_ref, imag_ref, leave_ref, vr, vi, gap, inputs_ready)
    fields(
        real_ref, imag_ref, rotation_ref, vr, vi, rotations,
        potential_ref, left_ref, right_ref, send, got, back, fin,
        send_sem, recv_sem, own_sem, small_send, small_recv, small_own,
        lambda: pl.semaphore_wait(barrier, PARTS - 1 + BANDS - 1), ready(2, 3), ready(4),
    )
    to_scalars = pltpu.make_async_copy(rotations, factors, small_own.at[1])
    to_scalars.start()
    pick(leave_ref, wave_ref, index_ref, applied_ref, vr, vi)
    to_scalars.wait()
    rotate(
        applied_ref, factors, order_ref, out_ref, window, mixed,
        first_send, first_recv, relay_send, relay_recv, out_send, out_recv, band_own,
    )


def shards(wave_coeffs, potential, sphere_index, rotation, panel_order):
    f32 = jnp.float32
    bf16 = jnp.bfloat16
    values = wave_coeffs.reshape(2, PACKED, 128).transpose(1, 0, 2).reshape(2 * PACKED, 128)
    index = sphere_index.reshape(PACKED, 128)
    left, right = left_tables(), right_tables()
    exchange_buffer = pltpu.VMEM((GROUPS * GROUP_ROWS, 128), f32)
    grid_buffer = pltpu.VMEM((GRID_ROWS, 128), f32)
    dma = pltpu.SemaphoreType.DMA

    def wide(kind):
        return pltpu.VMEM((GUARD + GRID_ROWS, 128), kind)

    out = pl.pallas_call(
        whole_kernel,
        out_shape=jax.ShapeDtypeStruct((OUT_LOCAL, 2 * PACKED, 128), f32),
        in_specs=[HBM_SPEC, HBM_SPEC, HBM_SPEC, VMEM_SPEC, SMEM_SPEC, HBM_SPEC, HBM_SPEC],
        out_specs=HBM_SPEC,
        scratch_shapes=[
            pltpu.VMEM((PACKED, 128), jnp.int32),
            pltpu.VMEM((2 * PACKED, 128), bf16),
            pltpu.VMEM((2 * PACKED, 128), f32),
            pltpu.VMEM(potential.shape, f32),
            pltpu.VMEM(left.shape, bf16),
            pltpu.VMEM(right.shape, bf16),
            grid_buffer,
            grid_buffer,
            pltpu.VMEM((GRID_ROWS, 128), jnp.int32),
            wide(f32),
            wide(f32),
            wide(jnp.int32),
        ]
        + [exchange_buffer] * 4
        + [
            pltpu.VMEM((PARTS, 2, 64), f32),
            pltpu.SMEM((PARTS, 2, 64), f32),
            pltpu.VMEM((2 * PACKED, 128), f32),
            pltpu.VMEM((PIECES, BANDS, HALF, 128), f32),
            pltpu.VMEM((PIECES, CHIPS, OUT_LOCAL, HALF, 128), f32),
            dma((5,)),
            dma((2, GROUPS, PARTS)),
            dma((2, GROUPS, PARTS)),
            dma((2, GROUPS)),
            dma((PARTS,)),
            dma((PARTS,)),
            dma((2,)),
        ]
        + [dma((PIECES, CHIPS))] * 2
        + [dma((PIECES,))] * 2
        + [dma((PIECES, CHIPS))] * 2
        + [dma((2, PIECES))],
        compiler_params=pltpu.CompilerParams(
            vmem_limit_bytes=VMEM_BYTES, collective_id=0, has_side_effects=True
        ),
        name="whole",
    )(index, values, potential, rotation, panel_order, jnp.asarray(left), jnp.asarray(right))
    return out.reshape(OUT_LOCAL, PACKED, 2, 128).transpose(0, 2, 1, 3).reshape(OUT_LOCAL, 2, PACKED * 128)


def solution(mesh):
    return jax.shard_map(
        shards,
        mesh=mesh,
        in_specs=(P("band", None, "pw"), P(None, "pw"), P("pw"), P("pw", None), P()),
        out_specs=P("band", None, "pw"),
        check_vma=False,
    )
```

```python
import math

import jax
import jax.numpy as jnp
import numpy as np
from jax import lax
from jax.experimental import pallas as pl
from jax.experimental.pallas import tpu as pltpu
from jax.sharding import PartitionSpec as P
import ml_dtypes

NG = 96
PARTS = 8
PLANES = NG // PARTS
GRID_ROWS = PLANES * NG
GROUPS = 3
SENT = 72
GROUP_ROWS = PARTS * SENT
PACKED = 480
CHIPS = 8
CUBE = ((4, (0, 1, 3, 2)), (1, (0, 3, 4, 7)), (3, (0, 1, 4, 5)))
PIECES = len(CUBE)
PARTED = 4
CHUNK = 2 * PACKED // PIECES // PARTED
HALF = CHUNK // 2
BANDS = 16
OUT_LOCAL = 4
GUARD = 512
BLOCK = 96
FLAG = 1 << 20
MESH = pl.DeviceIdType.MESH
VMEM_SPEC = pl.BlockSpec(memory_space=pltpu.VMEM)
SMEM_SPEC = pl.BlockSpec(memory_space=pltpu.SMEM)
HBM_SPEC = pl.BlockSpec(memory_space=pltpu.HBM)
VMEM_BYTES = 60 * 1024 * 1024


def split_table(table):
    high = table.astype(ml_dtypes.bfloat16)
    low = (table - high.astype(np.float64)).astype(ml_dtypes.bfloat16)
    return np.stack([high, low])


def stacked_table(direction, rows, columns):
    row_part, row_at = np.array(rows).T
    column_part, column_at = np.array(columns).T
    angles = 2.0 * math.pi / NG * (np.outer(row_at, column_at) % NG)
    cosines = np.cos(angles) / math.sqrt(NG)
    sines = direction * np.sin(angles) / math.sqrt(NG)
    same = row_part[:, None] == column_part[None, :]
    signs = np.where(row_part == 0, -1.0, 1.0)[:, None]
    return np.where(same, cosines, signs * sines)


def orders():
    natural = [(p, n) for p in range(2) for n in range(NG)]
    sent_y = [(p, PLANES * d + b) for p in range(2) for b in range(PLANES) for d in range(PARTS)]
    got_x = [
        (p, PLANES * s + 4 * g + t)
        for t in range(4) for g in range(GROUPS) for s in range(PARTS) for p in range(2)
    ]
    back_x = [
        (p, PLANES * e + 4 * g + t)
        for t in range(4) for e in range(PARTS) for g in range(GROUPS) for p in range(2)
    ]
    fin_y = [
        (p, PLANES * s + 4 * h + b)
        for p in range(2) for b in range(4) for h in range(GROUPS) for s in range(PARTS)
    ]
    return natural, sent_y, got_x, back_x, fin_y


def left_tables():
    natural, sent_y, got_x, back_x, fin_y = orders()
    return np.stack([
        split_table(stacked_table(1.0, sent_y, natural)),
        split_table(stacked_table(1.0, natural, got_x)),
        split_table(stacked_table(-1.0, back_x, natural)),
        split_table(stacked_table(-1.0, natural, fin_y)),
    ])


def right_tables():
    natural = orders()[0]
    stack = []
    for direction in (1.0, -1.0):
        table = stacked_table(direction, natural, natural).T
        wide = np.zeros((256, 256))
        for p in range(2):
            for q in range(2):
                wide[128 * p : 128 * p + NG, 128 * q : 128 * q + NG] = table[
                    NG * p : NG * p + NG, NG * q : NG * q + NG
                ]
        stack.append(split_table(wide))
    return np.stack(stack)


def split(value):
    high = value.astype(jnp.bfloat16)
    return high, (value - high.astype(jnp.float32)).astype(jnp.bfloat16)


def dot(a, b):
    return jnp.dot(a, b, preferred_element_type=jnp.float32)


def left_transform(table_ref, which, field):
    high, low = split(field)
    return (
        dot(table_ref[which, 0], high) + dot(table_ref[which, 0], low) + dot(table_ref[which, 1], high)
    )


def right_transform(table_ref, which, field):
    high, low = split(field)
    return (
        dot(high, table_ref[which, 0]) + dot(low, table_ref[which, 0]) + dot(high, table_ref[which, 1])
    )


def cell_of(index):
    line = ((index.astype(jnp.float32) + 0.5) * (1.0 / NG)).astype(jnp.int32)
    return line, index - NG * line


def along(value, lanes):
    return jnp.take_along_axis(value, lanes, axis=1, mode="promise_in_bounds")


def pack_fourth(lane, base, fourth, t):
    return jnp.where(lane < NG, base, pltpu.roll(fourth, NG - 32 * t, 1))


def unpack_fourth(lane, first, second, third):
    return jnp.where(
        lane < 32,
        pltpu.roll(first, 32, 1),
        jnp.where(lane < 64, pltpu.roll(second, 64, 1), pltpu.roll(third, 96, 1)),
    )


def spread(index_ref, wave_ref, real_ref, imag_ref, leave_ref, vr, vi, gap, ready):
    first_line = lax.axis_index("pw") * GRID_ROWS
    lane = lax.broadcasted_iota(jnp.int32, (BLOCK, 128), 1)
    rows = lax.broadcasted_iota(jnp.int32, (BLOCK, 128), 0)
    gap[...] = jnp.zeros_like(gap)
    for ref in (vr, vi):
        ref[pl.ds(0, GUARD), :] = jnp.zeros((GUARD, 128), jnp.float32)
        ref[pl.ds(GUARD + PACKED, GRID_ROWS - PACKED), :] = jnp.zeros((GRID_ROWS - PACKED, 128), jnp.float32)
    ready()
    for step in range(PACKED // BLOCK):
        base = step * BLOCK
        line, z = cell_of(index_ref[pl.ds(base, BLOCK), :])
        position = (rows + base) * 128 + lane
        at = pl.ds(GUARD + base, BLOCK)
        gap[at, :] = ((line - first_line) * 128 + z - position) | FLAG
        vr[at, :] = wave_ref[pl.ds(2 * base, BLOCK, stride=2), :]
        vi[at, :] = wave_ref[pl.ds(2 * base + 1, BLOCK, stride=2), :]

    for bit in range(16, 6, -1):
        shift = 1 << bit
        reach = min(PACKED + sum(1 << k for k in range(bit, 17)) // 128 + 1, GRID_ROWS)
        for step in reversed(range(GRID_ROWS // BLOCK)):
            base = step * BLOCK
            leave_at = pl.ds(base, BLOCK)
            if base >= reach:
                if bit == 16:
                    leave_ref[leave_at, :] = jnp.zeros((BLOCK, 128), jnp.int32)
                continue
            here = pl.ds(GUARD + base, BLOCK)
            there = pl.ds(GUARD + base - shift // 128, BLOCK)
            own = [ref[here, :] for ref in (gap, vr, vi)]
            other = [ref[there, :] for ref in (gap, vr, vi)]
            arrives = (other[0] & shift) != 0
            leaves = own[0] & shift
            held = jnp.where(arrives, other[0], jnp.where(leaves != 0, 0, own[0]))
            leaves = leaves if bit == 16 else leave_ref[leave_at, :] | leaves
            leave_ref[leave_at, :] = leaves if bit > 7 else leaves | (held & 127)
            gap[here, :] = held
            for k, ref in ((1, vr), (2, vi)):
                ref[here, :] = jnp.where(arrives, other[k], own[k])

    for bit in range(6, -1, -1):
        shift = 1 << bit
        stay = lane < 128 - shift
        for step in reversed(range(GRID_ROWS // BLOCK)):
            here = pl.ds(GUARD + step * BLOCK, BLOCK)
            before = pl.ds(GUARD + step * BLOCK - 1, BLOCK)
            own = gap[here, :]
            other = pltpu.roll(jnp.where(stay, own, gap[before, :]), shift, 1)
            held = jnp.where((other & shift) != 0, other, jnp.where((own & shift) != 0, 0, own))
            if bit:
                gap[here, :] = held
                continue
            moved = held & 127
            source = (lane - moved) & 127
            filled = (held & FLAG) != 0
            at = pl.ds(step * BLOCK, BLOCK)
            for ref, target in ((vr, real_ref), (vi, imag_ref)):
                value = jnp.where(lane >= moved, along(ref[here, :], source), along(ref[before, :], source))
                target[at, :] = jnp.where(filled, value, 0.0)


def fields(
    real_ref, imag_ref, rotation_ref, out_real, out_imag, rotations,
    potential_ref, left_ref, right_ref, send, got, back, fin,
    send_sem, recv_sem, own_sem, small_send, small_recv, small_own, enter, tables_ready, potential_ready,
):
    me = lax.axis_index("pw")
    peers = [lax.rem(me + turn, PARTS) for turn in range(PARTS)]
    def start_group(phase, group, source, target):
        copies = []
        for turn, peer in enumerate(peers):
            from_rows = pl.ds(pl.multiple_of(group * GROUP_ROWS + peer * SENT, SENT), SENT)
            to_rows = pl.ds(pl.multiple_of(group * GROUP_ROWS + me * SENT, SENT), SENT)
            if turn:
                copy = pltpu.make_async_remote_copy(
                    src_ref=source.at[from_rows, :],
                    dst_ref=target.at[to_rows, :],
                    send_sem=send_sem.at[phase, group, turn],
                    recv_sem=recv_sem.at[phase, group, turn],
                    device_id={"pw": peer},
                    device_id_type=MESH,
                )
            else:
                copy = pltpu.make_async_copy(
                    source.at[from_rows, :], target.at[to_rows, :], own_sem.at[phase, group]
                )
            copy.start()
            copies.append(copy)
        return copies

    tables_ready()
    lane = lax.broadcasted_iota(jnp.int32, (2 * NG, 128), 1)
    first = []
    for g in range(GROUPS):
        planes = []
        for pair in range(2):
            stacked = []
            for t in (2 * pair, 2 * pair + 1):
                at = pl.ds((4 * g + t) * NG, NG)
                field = jnp.concatenate([real_ref[at, :], imag_ref[at, :]], axis=1).astype(jnp.bfloat16)
                field = dot(field, right_ref[0, 0]) + dot(field, right_ref[0, 1])
                stacked.append(jnp.concatenate([field[:, :128], field[:, 128:]], axis=0))
            both = left_transform(left_ref, 0, jnp.concatenate(stacked, axis=1))
            planes += [both[:, :128], both[:, 128:]]
        for t in range(3):
            packed = pack_fourth(lane, planes[t], planes[3], t)
            for p in range(2):
                for b in range(PLANES):
                    row = (p * PLANES + b) * PARTS
                    at = pl.ds(g * GROUP_ROWS + (p * 3 + t) * PLANES + b, PARTS, stride=SENT)
                    send[at, :] = packed[row : row + PARTS]
        if g == 0:
            enter()
        first += start_group(0, g, send, got)

    small = []
    for turn, peer in enumerate(peers):
        if turn:
            copy = pltpu.make_async_remote_copy(
                src_ref=rotation_ref,
                dst_ref=rotations.at[me],
                send_sem=small_send.at[turn],
                recv_sem=small_recv.at[turn],
                device_id={"pw": peer},
                device_id_type=MESH,
            )
        else:
            copy = pltpu.make_async_copy(rotation_ref, rotations.at[me], small_own.at[0])
        copy.start()
        small.append(copy)

    potential_ready()
    for copy in first:
        copy.wait()
    lane48 = lax.broadcasted_iota(jnp.int32, (48, 128), 1)
    second = []
    for group in range(GROUPS):
        for pair in range(2):
            stacked, local = [], []
            for b in (4 * group + 2 * pair, 4 * group + 2 * pair + 1):
                planes = [got[pl.ds(t * PLANES + b, 48, stride=36), :] for t in range(3)]
                planes.append(unpack_fourth(lane48, *planes))
                stacked.append(jnp.concatenate(planes, axis=0))
                offset = b * NG % 128
                start = b * NG - offset
                if offset + NG > 128:
                    part = pltpu.roll(potential_ref[:, start : start + 256], 256 - offset, 1)[:, :128]
                else:
                    part = potential_ref[:, start : start + 128]
                    if offset:
                        part = pltpu.roll(part, 128 - offset, 1)
                local.append(part)
            local = jnp.concatenate(local, axis=1)
            field = left_transform(left_ref, 1, jnp.concatenate(stacked, axis=1))
            field = jnp.concatenate([local, local], axis=0) * field
            field = left_transform(left_ref, 2, field)
            for column in range(2):
                planes = [field[48 * t : 48 * t + 48, 128 * column : 128 * column + 128] for t in range(4)]
                for t in range(3):
                    at = pl.ds(group * GROUP_ROWS + t * 4 + 2 * pair + column, 48, stride=PLANES)
                    back[at, :] = pack_fourth(lane48, planes[t], planes[3], t)
        second += start_group(1, group, back, fin)
    for copy in second + small:
        copy.wait()
    lane96 = lax.broadcasted_iota(jnp.int32, (NG, 128), 1)
    for g in range(GROUPS):
        parts = []
        for p in range(2):
            planes = [
                jnp.concatenate(
                    [
                        fin[pl.ds(g * 24 + p * PLANES + t * 4 + b, 24, stride=SENT), :]
                        for b in range(4)
                    ],
                    axis=0,
                )
                for t in range(3)
            ]
            planes.append(unpack_fourth(lane96, *planes))
            parts.append(planes)
        for pair in range(2):
            stacked = [
                jnp.concatenate([parts[0][t], parts[1][t]], axis=0) for t in (2 * pair, 2 * pair + 1)
            ]
            both = left_transform(left_ref, 3, jnp.concatenate(stacked, axis=1))
            for column in range(2):
                plane = both[:, 128 * column : 128 * column + 128]
                field = jnp.concatenate([plane[:NG], plane[NG:]], axis=1)
                field = right_transform(right_ref, 1, field)
                at = pl.ds((4 * g + 2 * pair + column) * NG, NG)
                out_real[at, :] = field[:, :128]
                out_imag[at, :] = field[:, 128:]


def pick(leave_ref, wave_ref, index_ref, applied_ref, vr, vi):
    lane = lax.broadcasted_iota(jnp.int32, (BLOCK, 128), 1)
    for step in range(GRID_ROWS // BLOCK):
        here = pl.ds(step * BLOCK, BLOCK)
        after = pl.ds(step * BLOCK + 1, BLOCK)
        source = lane + (leave_ref[here, :] & 127)
        inside = source < 128
        source = source & 127
        for ref in (vr, vi):
            ref[here, :] = jnp.where(inside, along(ref[here, :], source), along(ref[after, :], source))
    for bit in range(7, 17):
        shift = 1 << bit
        needed = PACKED + sum(1 << k for k in range(bit + 1, 17)) // 128 + 1
        for step in range(GRID_ROWS // BLOCK):
            base = step * BLOCK
            if base >= needed:
                continue
            here = pl.ds(base, BLOCK)
            there = pl.ds(base + shift // 128, BLOCK)
            arrives = (leave_ref[here, :] & shift) != 0
            for ref in (vr, vi):
                ref[here, :] = jnp.where(arrives, ref[there, :], ref[here, :])

    def signed_square(position):
        signed = jnp.where(position < NG // 2, position, position - NG).astype(jnp.float32)
        return signed * signed

    for step in range(PACKED // BLOCK):
        base = step * BLOCK
        line, z = cell_of(index_ref[pl.ds(base, BLOCK), :])
        x, y = cell_of(line)
        energy = 2.0 * (signed_square(x) + signed_square(y) + signed_square(z)) / float((NG // 2) ** 2)
        for part, ref in enumerate((vr, vi)):
            at = pl.ds(2 * base + part, BLOCK, stride=2)
            applied_ref[at, :] = energy * wave_ref[at, :] + ref[pl.ds(base, BLOCK), :]


def across(chip, mask):
    z, x = chip // 4, chip % 4
    x = (x, x + 1 - 2 * (x % 2), (x + 2) % 4, 3 - x)[mask % 4]
    return (1 - z if mask >= 4 else z) * 4 + x


def part_of(chip, piece):
    z, x = chip // 4, chip % 4
    near, far = (x + x // 2) % 2, x // 2
    return (near + 2 * far, far + 2 * z, near + 2 * z)[piece]


def rotate(
    applied_ref, rotations, order_ref, out_ref, window, mixed,
    first_send, first_recv, relay_send, relay_recv, out_send, out_recv, own_sem,
):
    band = lax.axis_index("band")
    chip, core = band // 2, band % 2
    cores = (core, 1 - core)

    def rows(which, piece, half):
        start = piece * PARTED * CHUNK + part_of(which, piece) * CHUNK + half * HALF
        return pl.ds(pl.multiple_of(start, HALF), HALF)

    def move(source, target, peer, turn, send, recv, own):
        if turn:
            copy = pltpu.make_async_remote_copy(
                src_ref=source,
                dst_ref=target,
                send_sem=send,
                recv_sem=recv,
                device_id={"band": peer},
                device_id_type=MESH,
            )
        else:
            copy = pltpu.make_async_copy(source, target, own)
        copy.start()
        return copy

    relayed, results = [], []
    sent = [[None] * CHIPS for _ in CUBE]
    for k in reversed(range(PARTED)):
        for piece, (_, masks) in enumerate(CUBE):
            peer = across(chip, masks[k])
            for c, half in enumerate(cores):
                turn = 2 * k + c
                sent[piece][turn] = move(
                    applied_ref.at[rows(peer, piece, half), :], window.at[piece, 2 * k + core],
                    peer * 2 + half, turn, first_send.at[piece, turn], first_recv.at[piece, turn],
                    own_sem.at[0, piece],
                )

    def relay(piece):
        sent[piece][0].wait()
        for copy in sent[piece][1:]:
            copy.wait_recv()
        relayed.append(move(
            window.at[piece, pl.ds(0, CHIPS)], window.at[piece, pl.ds(CHIPS, CHIPS)],
            across(chip, CUBE[piece][0]) * 2 + core, 1, relay_send.at[piece], relay_recv.at[piece], None,
        ))

    def panels_of(piece):
        shared, masks = CUBE[piece]
        panels = []
        for start in (chip, across(chip, shared)):
            for mask in masks:
                for c in range(2):
                    panel = order_ref[across(start, mask) * 2 + c]
                    panels.append((panel // 2, panel % 2))
        return panels

    def mix(piece, k, c, panels):
        peer = across(chip, CUBE[piece][1][k]) * 2 + cores[c]
        turn = 2 * k + c
        totals = [None] * OUT_LOCAL
        for i in range(BANDS):
            term = window[piece, i]
            for j in range(OUT_LOCAL):
                factor = rotations[panels[i][0], panels[i][1], peer * OUT_LOCAL + j]
                totals[j] = factor * term if i == 0 else totals[j] + factor * term
        for j in range(OUT_LOCAL):
            mixed[piece, turn, j] = totals[j]
        results.append(move(
            mixed.at[piece, turn], out_ref.at[piece, part_of(chip, piece), core],
            peer, turn, out_send.at[piece, turn], out_recv.at[piece, turn], own_sem.at[1, piece],
        ))

    for piece in range(PIECES):
        relay(piece)
    panels = [panels_of(piece) for piece in range(PIECES)]
    for k in reversed(range(PARTED)):
        for piece in range(PIECES):
            if k == PARTED - 1:
                relayed[piece].wait_recv()
            for c in (1, 0):
                mix(piece, k, c, panels[piece])
    for copies in sent:
        for copy in copies[1:]:
            copy.wait_send()
    for copy in relayed:
        copy.wait_send()
    for copy in results:
        copy.wait()


def whole_kernel(
    index_hbm, wave_hbm, potential_hbm, rotation_ref, order_ref, left_hbm, right_hbm,
    out_ref,
    index_ref, narrow_ref, wave_ref, potential_ref, left_ref, right_ref,
    real_ref, imag_ref, leave_ref, vr, vi, gap, send, got, back, fin, rotations, factors, applied_ref, window, mixed,
    load_sem, send_sem, recv_sem, own_sem, small_send, small_recv, small_own,
    first_send, first_recv, relay_send, relay_recv, out_send, out_recv, band_own,
):
    loads = [
        pltpu.make_async_copy(source, target, load_sem.at[k])
        for k, (source, target) in enumerate((
            (index_hbm, index_ref), (wave_hbm, narrow_ref), (right_hbm, right_ref),
            (left_hbm, left_ref), (potential_hbm, potential_ref),
        ))
    ]
    for load in loads:
        load.start()
    me, band = lax.axis_index("pw"), lax.axis_index("band")
    barrier = pltpu.get_barrier_semaphore()
    for turn in range(1, PARTS):
        pl.semaphore_signal(
            barrier, inc=1, device_id={"pw": lax.rem(me + turn, PARTS)}, device_id_type=MESH
        )
    for turn in range(1, BANDS):
        peer = lax.rem(band + turn, BANDS)
        pl.semaphore_signal(barrier, inc=1, device_id={"band": peer}, device_id_type=MESH)

    def ready(*which):
        def wait():
            for k in which:
                loads[k].wait()

        return wait

    def inputs_ready():
        ready(0, 1)()
        wave_ref[...] = narrow_ref[...].astype(jnp.float32)

    spread(index_ref, wave_ref, real_ref, imag_ref, leave_ref, vr, vi, gap, inputs_ready)
    fields(
        real_ref, imag_ref, rotation_ref, vr, vi, rotations,
        potential_ref, left_ref, right_ref, send, got, back, fin,
        send_sem, recv_sem, own_sem, small_send, small_recv, small_own,
        lambda: pl.semaphore_wait(barrier, PARTS - 1 + BANDS - 1), ready(2, 3), ready(4),
    )
    to_scalars = pltpu.make_async_copy(rotations, factors, small_own.at[1])
    to_scalars.start()
    pick(leave_ref, wave_ref, index_ref, applied_ref, vr, vi)
    to_scalars.wait()
    rotate(
        applied_ref, factors, order_ref, out_ref, window, mixed,
        first_send, first_recv, relay_send, relay_recv, out_send, out_recv, band_own,
    )


def shards(wave_coeffs, potential, sphere_index, rotation, panel_order):
    f32 = jnp.float32
    bf16 = jnp.bfloat16
    values = wave_coeffs.reshape(2, PACKED, 128).transpose(1, 0, 2).reshape(2 * PACKED, 128)
    index = sphere_index.reshape(PACKED, 128)
    left, right = left_tables(), right_tables()
    exchange_buffer = pltpu.VMEM((GROUPS * GROUP_ROWS, 128), f32)
    grid_buffer = pltpu.VMEM((GRID_ROWS, 128), f32)
    dma = pltpu.SemaphoreType.DMA

    def wide(kind):
        return pltpu.VMEM((GUARD + GRID_ROWS, 128), kind)

    out = pl.pallas_call(
        whole_kernel,
        out_shape=jax.ShapeDtypeStruct((PIECES, PARTED, 2, OUT_LOCAL, HALF, 128), f32),
        in_specs=[HBM_SPEC, HBM_SPEC, HBM_SPEC, VMEM_SPEC, SMEM_SPEC, HBM_SPEC, HBM_SPEC],
        out_specs=HBM_SPEC,
        scratch_shapes=[
            pltpu.VMEM((PACKED, 128), jnp.int32),
            pltpu.VMEM((2 * PACKED, 128), bf16),
            pltpu.VMEM((2 * PACKED, 128), f32),
            pltpu.VMEM(potential.shape, f32),
            pltpu.VMEM(left.shape, bf16),
            pltpu.VMEM(right.shape, bf16),
            grid_buffer,
            grid_buffer,
            pltpu.VMEM((GRID_ROWS, 128), jnp.int32),
            wide(f32),
            wide(f32),
            wide(jnp.int32),
        ]
        + [exchange_buffer] * 4
        + [
            pltpu.VMEM((PARTS, 2, 64), f32),
            pltpu.SMEM((PARTS, 2, 64), f32),
            pltpu.VMEM((2 * PACKED, 128), f32),
            pltpu.VMEM((PIECES, BANDS, HALF, 128), f32),
            pltpu.VMEM((PIECES, CHIPS, OUT_LOCAL, HALF, 128), f32),
            dma((5,)),
            dma((2, GROUPS, PARTS)),
            dma((2, GROUPS, PARTS)),
            dma((2, GROUPS)),
            dma((PARTS,)),
            dma((PARTS,)),
            dma((2,)),
        ]
        + [dma((PIECES, CHIPS))] * 2
        + [dma((PIECES,))] * 2
        + [dma((PIECES, CHIPS))] * 2
        + [dma((2, PIECES))],
        compiler_params=pltpu.CompilerParams(
            vmem_limit_bytes=VMEM_BYTES, collective_id=0, has_side_effects=True
        ),
        name="whole",
    )(index, values, potential, rotation, panel_order, jnp.asarray(left), jnp.asarray(right))
    out = out.transpose(3, 0, 1, 2, 4, 5)
    return out.reshape(OUT_LOCAL, PACKED, 2, 128).transpose(0, 2, 1, 3).reshape(OUT_LOCAL, 2, PACKED * 128)


def solution(mesh):
    return jax.shard_map(
        shards,
        mesh=mesh,
        in_specs=(P("band", None, "pw"), P(None, "pw"), P("pw"), P("pw", None), P()),
        out_specs=P("band", None, "pw"),
        check_vma=False,
    )
```

```python
import math

import jax
import jax.numpy as jnp
import numpy as np
from jax import lax
from jax.experimental import pallas as pl
from jax.experimental.pallas import tpu as pltpu
from jax.sharding import PartitionSpec as P
import ml_dtypes

NG = 96
PARTS = 8
PLANES = NG // PARTS
GRID_ROWS = PLANES * NG
GROUPS = 3
SENT = 72
GROUP_ROWS = PARTS * SENT
PACKED = 480
CHIPS = 8
CUBE = ((4, (0, 1, 3, 2)), (1, (0, 3, 4, 7)), (3, (0, 1, 4, 5)))
PIECES = len(CUBE)
PARTED = 4
CHUNK = 2 * PACKED // PIECES // PARTED
HALF = CHUNK // 2
BANDS = 16
OUT_LOCAL = 4
GUARD = 512
BLOCK = 96
FLAG = 1 << 20
MESH = pl.DeviceIdType.MESH
VMEM_SPEC = pl.BlockSpec(memory_space=pltpu.VMEM)
SMEM_SPEC = pl.BlockSpec(memory_space=pltpu.SMEM)
HBM_SPEC = pl.BlockSpec(memory_space=pltpu.HBM)
VMEM_BYTES = 60 * 1024 * 1024


def split_table(table):
    high = table.astype(ml_dtypes.bfloat16)
    low = (table - high.astype(np.float64)).astype(ml_dtypes.bfloat16)
    return np.stack([high, low])


def stacked_table(direction, rows, columns):
    row_part, row_at = np.array(rows).T
    column_part, column_at = np.array(columns).T
    angles = 2.0 * math.pi / NG * (np.outer(row_at, column_at) % NG)
    cosines = np.cos(angles) / math.sqrt(NG)
    sines = direction * np.sin(angles) / math.sqrt(NG)
    same = row_part[:, None] == column_part[None, :]
    signs = np.where(row_part == 0, -1.0, 1.0)[:, None]
    return np.where(same, cosines, signs * sines)


def orders():
    natural = [(p, n) for p in range(2) for n in range(NG)]
    sent_y = [(p, PLANES * d + b) for p in range(2) for b in range(PLANES) for d in range(PARTS)]
    got_x = [
        (p, PLANES * s + 4 * g + t)
        for t in range(4) for g in range(GROUPS) for s in range(PARTS) for p in range(2)
    ]
    back_x = [
        (p, PLANES * e + 4 * g + t)
        for t in range(4) for e in range(PARTS) for g in range(GROUPS) for p in range(2)
    ]
    fin_y = [
        (p, PLANES * s + 4 * h + b)
        for p in range(2) for b in range(4) for h in range(GROUPS) for s in range(PARTS)
    ]
    return natural, sent_y, got_x, back_x, fin_y


def left_tables():
    natural, sent_y, got_x, back_x, fin_y = orders()
    return np.stack([
        split_table(stacked_table(1.0, sent_y, natural)),
        split_table(stacked_table(1.0, natural, got_x)),
        split_table(stacked_table(-1.0, back_x, natural)),
        split_table(stacked_table(-1.0, natural, fin_y)),
    ])


def right_tables():
    natural = orders()[0]
    stack = []
    for direction in (1.0, -1.0):
        table = stacked_table(direction, natural, natural).T
        wide = np.zeros((256, 256))
        for p in range(2):
            for q in range(2):
                wide[128 * p : 128 * p + NG, 128 * q : 128 * q + NG] = table[
                    NG * p : NG * p + NG, NG * q : NG * q + NG
                ]
        stack.append(split_table(wide))
    return np.stack(stack)


def split(value):
    high = value.astype(jnp.bfloat16)
    return high, (value - high.astype(jnp.float32)).astype(jnp.bfloat16)


def dot(a, b):
    return jnp.dot(a, b, preferred_element_type=jnp.float32)


def left_transform(table_ref, which, field):
    high, low = split(field)
    return (
        dot(table_ref[which, 0], high) + dot(table_ref[which, 0], low) + dot(table_ref[which, 1], high)
    )


def right_transform(table_ref, which, field):
    high, low = split(field)
    return (
        dot(high, table_ref[which, 0]) + dot(low, table_ref[which, 0]) + dot(high, table_ref[which, 1])
    )


def cell_of(index):
    line = ((index.astype(jnp.float32) + 0.5) * (1.0 / NG)).astype(jnp.int32)
    return line, index - NG * line


def along(value, lanes):
    return jnp.take_along_axis(value, lanes, axis=1, mode="promise_in_bounds")


def pack_fourth(lane, base, fourth, t):
    return jnp.where(lane < NG, base, pltpu.roll(fourth, NG - 32 * t, 1))


def unpack_fourth(lane, first, second, third):
    return jnp.where(
        lane < 32,
        pltpu.roll(first, 32, 1),
        jnp.where(lane < 64, pltpu.roll(second, 64, 1), pltpu.roll(third, 96, 1)),
    )


def spread(index_ref, wave_ref, real_ref, imag_ref, leave_ref, vr, vi, gap, ready):
    first_line = lax.axis_index("pw") * GRID_ROWS
    lane = lax.broadcasted_iota(jnp.int32, (BLOCK, 128), 1)
    rows = lax.broadcasted_iota(jnp.int32, (BLOCK, 128), 0)
    gap[...] = jnp.zeros_like(gap)
    for ref in (vr, vi):
        ref[pl.ds(0, GUARD), :] = jnp.zeros((GUARD, 128), jnp.float32)
        ref[pl.ds(GUARD + PACKED, GRID_ROWS - PACKED), :] = jnp.zeros((GRID_ROWS - PACKED, 128), jnp.float32)
    ready()
    for step in range(PACKED // BLOCK):
        base = step * BLOCK
        line, z = cell_of(index_ref[pl.ds(base, BLOCK), :])
        position = (rows + base) * 128 + lane
        at = pl.ds(GUARD + base, BLOCK)
        gap[at, :] = ((line - first_line) * 128 + z - position) | FLAG
        vr[at, :] = wave_ref[pl.ds(2 * base, BLOCK, stride=2), :]
        vi[at, :] = wave_ref[pl.ds(2 * base + 1, BLOCK, stride=2), :]

    for bit in range(16, 6, -1):
        shift = 1 << bit
        reach = min(PACKED + sum(1 << k for k in range(bit, 17)) // 128 + 1, GRID_ROWS)
        for step in reversed(range(GRID_ROWS // BLOCK)):
            base = step * BLOCK
            leave_at = pl.ds(base, BLOCK)
            if base >= reach:
                if bit == 16:
                    leave_ref[leave_at, :] = jnp.zeros((BLOCK, 128), jnp.int32)
                continue
            here = pl.ds(GUARD + base, BLOCK)
            there = pl.ds(GUARD + base - shift // 128, BLOCK)
            own = [ref[here, :] for ref in (gap, vr, vi)]
            other = [ref[there, :] for ref in (gap, vr, vi)]
            arrives = (other[0] & shift) != 0
            leaves = own[0] & shift
            held = jnp.where(arrives, other[0], jnp.where(leaves != 0, 0, own[0]))
            leaves = leaves if bit == 16 else leave_ref[leave_at, :] | leaves
            leave_ref[leave_at, :] = leaves if bit > 7 else leaves | (held & 127)
            gap[here, :] = held
            for k, ref in ((1, vr), (2, vi)):
                ref[here, :] = jnp.where(arrives, other[k], own[k])

    for bit in range(6, -1, -1):
        shift = 1 << bit
        stay = lane < 128 - shift
        for step in reversed(range(GRID_ROWS // BLOCK)):
            here = pl.ds(GUARD + step * BLOCK, BLOCK)
            before = pl.ds(GUARD + step * BLOCK - 1, BLOCK)
            own = gap[here, :]
            other = pltpu.roll(jnp.where(stay, own, gap[before, :]), shift, 1)
            held = jnp.where((other & shift) != 0, other, jnp.where((own & shift) != 0, 0, own))
            if bit:
                gap[here, :] = held
                continue
            moved = held & 127
            source = (lane - moved) & 127
            filled = (held & FLAG) != 0
            at = pl.ds(step * BLOCK, BLOCK)
            for ref, target in ((vr, real_ref), (vi, imag_ref)):
                value = jnp.where(lane >= moved, along(ref[here, :], source), along(ref[before, :], source))
                target[at, :] = jnp.where(filled, value, 0.0)


def fields(
    real_ref, imag_ref, rotation_ref, out_real, out_imag, rotations,
    potential_ref, left_ref, right_ref, send, got, back, fin,
    send_sem, recv_sem, own_sem, small_send, small_recv, small_own, enter, tables_ready, potential_ready,
):
    me = lax.axis_index("pw")
    peers = [lax.rem(me + turn, PARTS) for turn in range(PARTS)]
    def start_group(phase, group, source, target):
        copies = []
        for turn, peer in enumerate(peers):
            from_rows = pl.ds(pl.multiple_of(group * GROUP_ROWS + peer * SENT, SENT), SENT)
            to_rows = pl.ds(pl.multiple_of(group * GROUP_ROWS + me * SENT, SENT), SENT)
            if turn:
                copy = pltpu.make_async_remote_copy(
                    src_ref=source.at[from_rows, :],
                    dst_ref=target.at[to_rows, :],
                    send_sem=send_sem.at[phase, group, turn],
                    recv_sem=recv_sem.at[phase, group, turn],
                    device_id={"pw": peer},
                    device_id_type=MESH,
                )
            else:
                copy = pltpu.make_async_copy(
                    source.at[from_rows, :], target.at[to_rows, :], own_sem.at[phase, group]
                )
            copy.start()
            copies.append(copy)
        return copies

    tables_ready()
    lane = lax.broadcasted_iota(jnp.int32, (2 * NG, 128), 1)
    first = []
    for g in range(GROUPS):
        planes = []
        for pair in range(2):
            stacked = []
            for t in (2 * pair, 2 * pair + 1):
                at = pl.ds((4 * g + t) * NG, NG)
                field = jnp.concatenate([real_ref[at, :], imag_ref[at, :]], axis=1).astype(jnp.bfloat16)
                field = dot(field, right_ref[0, 0]) + dot(field, right_ref[0, 1])
                stacked.append(jnp.concatenate([field[:, :128], field[:, 128:]], axis=0))
            both = left_transform(left_ref, 0, jnp.concatenate(stacked, axis=1))
            planes += [both[:, :128], both[:, 128:]]
        for t in range(3):
            packed = pack_fourth(lane, planes[t], planes[3], t)
            for p in range(2):
                for b in range(PLANES):
                    row = (p * PLANES + b) * PARTS
                    at = pl.ds(g * GROUP_ROWS + (p * 3 + t) * PLANES + b, PARTS, stride=SENT)
                    send[at, :] = packed[row : row + PARTS]
        if g == 0:
            enter()
        first += start_group(0, g, send, got)

    small = []
    for turn, peer in enumerate(peers):
        if turn:
            copy = pltpu.make_async_remote_copy(
                src_ref=rotation_ref,
                dst_ref=rotations.at[me],
                send_sem=small_send.at[turn],
                recv_sem=small_recv.at[turn],
                device_id={"pw": peer},
                device_id_type=MESH,
            )
        else:
            copy = pltpu.make_async_copy(rotation_ref, rotations.at[me], small_own.at[0])
        copy.start()
        small.append(copy)

    potential_ready()
    for copy in first:
        copy.wait()
    lane48 = lax.broadcasted_iota(jnp.int32, (48, 128), 1)
    second = []
    for group in range(GROUPS):
        for pair in range(2):
            stacked, local = [], []
            for b in (4 * group + 2 * pair, 4 * group + 2 * pair + 1):
                planes = [got[pl.ds(t * PLANES + b, 48, stride=36), :] for t in range(3)]
                planes.append(unpack_fourth(lane48, *planes))
                stacked.append(jnp.concatenate(planes, axis=0))
                offset = b * NG % 128
                start = b * NG - offset
                if offset + NG > 128:
                    part = pltpu.roll(potential_ref[:, start : start + 256], 256 - offset, 1)[:, :128]
                else:
                    part = potential_ref[:, start : start + 128]
                    if offset:
                        part = pltpu.roll(part, 128 - offset, 1)
                local.append(part)
            local = jnp.concatenate(local, axis=1)
            field = left_transform(left_ref, 1, jnp.concatenate(stacked, axis=1))
            field = jnp.concatenate([local, local], axis=0) * field
            field = left_transform(left_ref, 2, field)
            for column in range(2):
                planes = [field[48 * t : 48 * t + 48, 128 * column : 128 * column + 128] for t in range(4)]
                for t in range(3):
                    at = pl.ds(group * GROUP_ROWS + t * 4 + 2 * pair + column, 48, stride=PLANES)
                    back[at, :] = pack_fourth(lane48, planes[t], planes[3], t)
        second += start_group(1, group, back, fin)
    for copy in second + small:
        copy.wait()
    lane96 = lax.broadcasted_iota(jnp.int32, (NG, 128), 1)
    for g in range(GROUPS):
        parts = []
        for p in range(2):
            planes = [
                jnp.concatenate(
                    [
                        fin[pl.ds(g * 24 + p * PLANES + t * 4 + b, 24, stride=SENT), :]
                        for b in range(4)
                    ],
                    axis=0,
                )
                for t in range(3)
            ]
            planes.append(unpack_fourth(lane96, *planes))
            parts.append(planes)
        for pair in range(2):
            stacked = [
                jnp.concatenate([parts[0][t], parts[1][t]], axis=0) for t in (2 * pair, 2 * pair + 1)
            ]
            both = left_transform(left_ref, 3, jnp.concatenate(stacked, axis=1))
            for column in range(2):
                plane = both[:, 128 * column : 128 * column + 128]
                field = jnp.concatenate([plane[:NG], plane[NG:]], axis=1)
                field = right_transform(right_ref, 1, field)
                at = pl.ds((4 * g + 2 * pair + column) * NG, NG)
                out_real[at, :] = field[:, :128]
                out_imag[at, :] = field[:, 128:]


def pick(leave_ref, wave_ref, index_ref, applied_ref, vr, vi):
    lane = lax.broadcasted_iota(jnp.int32, (BLOCK, 128), 1)
    for step in range(GRID_ROWS // BLOCK):
        here = pl.ds(step * BLOCK, BLOCK)
        after = pl.ds(step * BLOCK + 1, BLOCK)
        source = lane + (leave_ref[here, :] & 127)
        inside = source < 128
        source = source & 127
        for ref in (vr, vi):
            ref[here, :] = jnp.where(inside, along(ref[here, :], source), along(ref[after, :], source))
    for bit in range(7, 17):
        shift = 1 << bit
        needed = PACKED + sum(1 << k for k in range(bit + 1, 17)) // 128 + 1
        for step in range(GRID_ROWS // BLOCK):
            base = step * BLOCK
            if base >= needed:
                continue
            here = pl.ds(base, BLOCK)
            there = pl.ds(base + shift // 128, BLOCK)
            arrives = (leave_ref[here, :] & shift) != 0
            for ref in (vr, vi):
                ref[here, :] = jnp.where(arrives, ref[there, :], ref[here, :])

    def signed_square(position):
        signed = jnp.where(position < NG // 2, position, position - NG).astype(jnp.float32)
        return signed * signed

    def finish(step):
        base = step * BLOCK
        line, z = cell_of(index_ref[pl.ds(base, BLOCK), :])
        x, y = cell_of(line)
        energy = 2.0 * (signed_square(x) + signed_square(y) + signed_square(z)) / float((NG // 2) ** 2)
        for part, ref in enumerate((vr, vi)):
            at = pl.ds(2 * base + part, BLOCK, stride=2)
            applied_ref[at, :] = energy * wave_ref[at, :] + ref[pl.ds(base, BLOCK), :]

    return finish


def across(chip, mask):
    z, x = chip // 4, chip % 4
    x = (x, x + 1 - 2 * (x % 2), (x + 2) % 4, 3 - x)[mask % 4]
    return (1 - z if mask >= 4 else z) * 4 + x


def part_of(chip, piece):
    z, x = chip // 4, chip % 4
    near, far = (x + x // 2) % 2, x // 2
    return (near + 2 * far, far + 2 * z, near + 2 * z)[piece]


def rotate(
    finish, applied_ref, rotations, order_ref, out_ref, window, mixed,
    first_send, first_recv, relay_send, relay_recv, out_send, out_recv, own_sem,
):
    band = lax.axis_index("band")
    chip, core = band // 2, band % 2
    cores = (core, 1 - core)

    def rows(which, piece, half):
        start = piece * PARTED * CHUNK + part_of(which, piece) * CHUNK + half * HALF
        return pl.ds(pl.multiple_of(start, HALF), HALF)

    def move(source, target, peer, turn, send, recv, own):
        if turn:
            copy = pltpu.make_async_remote_copy(
                src_ref=source,
                dst_ref=target,
                send_sem=send,
                recv_sem=recv,
                device_id={"band": peer},
                device_id_type=MESH,
            )
        else:
            copy = pltpu.make_async_copy(source, target, own)
        copy.start()
        return copy

    relayed, results = [], []
    sent = [[None] * CHIPS for _ in CUBE]
    done = 0
    for piece, (_, masks) in enumerate(CUBE):
        while done * 2 * BLOCK < (piece + 1) * PARTED * CHUNK:
            finish(done)
            done += 1
        for k in reversed(range(PARTED)):
            peer = across(chip, masks[k])
            for c, half in enumerate(cores):
                turn = 2 * k + c
                sent[piece][turn] = move(
                    applied_ref.at[rows(peer, piece, half), :], window.at[piece, 2 * k + core],
                    peer * 2 + half, turn, first_send.at[piece, turn], first_recv.at[piece, turn],
                    own_sem.at[0, piece],
                )

    def relay(piece):
        sent[piece][0].wait()
        for copy in sent[piece][1:]:
            copy.wait_recv()
        relayed.append(move(
            window.at[piece, pl.ds(0, CHIPS)], window.at[piece, pl.ds(CHIPS, CHIPS)],
            across(chip, CUBE[piece][0]) * 2 + core, 1, relay_send.at[piece], relay_recv.at[piece], None,
        ))

    def panels_of(piece):
        shared, masks = CUBE[piece]
        panels = []
        for start in (chip, across(chip, shared)):
            for mask in masks:
                for c in range(2):
                    panel = order_ref[across(start, mask) * 2 + c]
                    panels.append((panel // 2, panel % 2))
        return panels

    def mix(piece, k, c, panels):
        peer = across(chip, CUBE[piece][1][k]) * 2 + cores[c]
        turn = 2 * k + c
        totals = [None] * OUT_LOCAL
        for i in range(BANDS):
            term = window[piece, i]
            for j in range(OUT_LOCAL):
                factor = rotations[panels[i][0], panels[i][1], peer * OUT_LOCAL + j]
                totals[j] = factor * term if i == 0 else totals[j] + factor * term
        for j in range(OUT_LOCAL):
            mixed[piece, turn, j] = totals[j]
        results.append(move(
            mixed.at[piece, turn], out_ref.at[piece, part_of(chip, piece), core],
            peer, turn, out_send.at[piece, turn], out_recv.at[piece, turn], own_sem.at[1, piece],
        ))

    for piece in range(PIECES):
        relay(piece)
    panels = [panels_of(piece) for piece in range(PIECES)]
    for k in reversed(range(PARTED)):
        for piece in range(PIECES):
            if k == PARTED - 1:
                relayed[piece].wait_recv()
            for c in (1, 0):
                mix(piece, k, c, panels[piece])
    for copies in sent:
        for copy in copies[1:]:
            copy.wait_send()
    for copy in relayed:
        copy.wait_send()
    for copy in results:
        copy.wait()


def whole_kernel(
    index_hbm, wave_hbm, potential_hbm, rotation_ref, order_ref, left_hbm, right_hbm,
    out_ref,
    index_ref, narrow_ref, wave_ref, potential_ref, left_ref, right_ref,
    real_ref, imag_ref, leave_ref, vr, vi, gap, send, got, back, fin, rotations, factors, applied_ref, window, mixed,
    load_sem, send_sem, recv_sem, own_sem, small_send, small_recv, small_own,
    first_send, first_recv, relay_send, relay_recv, out_send, out_recv, band_own,
):
    loads = [
        pltpu.make_async_copy(source, target, load_sem.at[k])
        for k, (source, target) in enumerate((
            (index_hbm, index_ref), (wave_hbm, narrow_ref), (right_hbm, right_ref),
            (left_hbm, left_ref), (potential_hbm, potential_ref),
        ))
    ]
    for load in loads:
        load.start()
    me, band = lax.axis_index("pw"), lax.axis_index("band")
    barrier = pltpu.get_barrier_semaphore()
    for turn in range(1, PARTS):
        pl.semaphore_signal(
            barrier, inc=1, device_id={"pw": lax.rem(me + turn, PARTS)}, device_id_type=MESH
        )
    for turn in range(1, BANDS):
        peer = lax.rem(band + turn, BANDS)
        pl.semaphore_signal(barrier, inc=1, device_id={"band": peer}, device_id_type=MESH)

    def ready(*which):
        def wait():
            for k in which:
                loads[k].wait()

        return wait

    def inputs_ready():
        ready(0, 1)()
        wave_ref[...] = narrow_ref[...].astype(jnp.float32)

    spread(index_ref, wave_ref, real_ref, imag_ref, leave_ref, vr, vi, gap, inputs_ready)
    fields(
        real_ref, imag_ref, rotation_ref, vr, vi, rotations,
        potential_ref, left_ref, right_ref, send, got, back, fin,
        send_sem, recv_sem, own_sem, small_send, small_recv, small_own,
        lambda: pl.semaphore_wait(barrier, PARTS - 1 + BANDS - 1), ready(2, 3), ready(4),
    )
    to_scalars = pltpu.make_async_copy(rotations, factors, small_own.at[1])
    to_scalars.start()
    finish = pick(leave_ref, wave_ref, index_ref, applied_ref, vr, vi)
    to_scalars.wait()
    rotate(
        finish, applied_ref, factors, order_ref, out_ref, window, mixed,
        first_send, first_recv, relay_send, relay_recv, out_send, out_recv, band_own,
    )


def shards(wave_coeffs, potential, sphere_index, rotation, panel_order):
    f32 = jnp.float32
    bf16 = jnp.bfloat16
    values = wave_coeffs.reshape(2, PACKED, 128).transpose(1, 0, 2).reshape(2 * PACKED, 128)
    index = sphere_index.reshape(PACKED, 128)
    left, right = left_tables(), right_tables()
    exchange_buffer = pltpu.VMEM((GROUPS * GROUP_ROWS, 128), f32)
    grid_buffer = pltpu.VMEM((GRID_ROWS, 128), f32)
    dma = pltpu.SemaphoreType.DMA

    def wide(kind):
        return pltpu.VMEM((GUARD + GRID_ROWS, 128), kind)

    out = pl.pallas_call(
        whole_kernel,
        out_shape=jax.ShapeDtypeStruct((PIECES, PARTED, 2, OUT_LOCAL, HALF, 128), f32),
        in_specs=[HBM_SPEC, HBM_SPEC, HBM_SPEC, VMEM_SPEC, SMEM_SPEC, HBM_SPEC, HBM_SPEC],
        out_specs=HBM_SPEC,
        scratch_shapes=[
            pltpu.VMEM((PACKED, 128), jnp.int32),
            pltpu.VMEM((2 * PACKED, 128), bf16),
            pltpu.VMEM((2 * PACKED, 128), f32),
            pltpu.VMEM(potential.shape, f32),
            pltpu.VMEM(left.shape, bf16),
            pltpu.VMEM(right.shape, bf16),
            grid_buffer,
            grid_buffer,
            pltpu.VMEM((GRID_ROWS, 128), jnp.int32),
            wide(f32),
            wide(f32),
            wide(jnp.int32),
        ]
        + [exchange_buffer] * 4
        + [
            pltpu.VMEM((PARTS, 2, 64), f32),
            pltpu.SMEM((PARTS, 2, 64), f32),
            pltpu.VMEM((2 * PACKED, 128), f32),
            pltpu.VMEM((PIECES, BANDS, HALF, 128), f32),
            pltpu.VMEM((PIECES, CHIPS, OUT_LOCAL, HALF, 128), f32),
            dma((5,)),
            dma((2, GROUPS, PARTS)),
            dma((2, GROUPS, PARTS)),
            dma((2, GROUPS)),
            dma((PARTS,)),
            dma((PARTS,)),
            dma((2,)),
        ]
        + [dma((PIECES, CHIPS))] * 2
        + [dma((PIECES,))] * 2
        + [dma((PIECES, CHIPS))] * 2
        + [dma((2, PIECES))],
        compiler_params=pltpu.CompilerParams(
            vmem_limit_bytes=VMEM_BYTES, collective_id=0, has_side_effects=True
        ),
        name="whole",
    )(index, values, potential, rotation, panel_order, jnp.asarray(left), jnp.asarray(right))
    out = out.transpose(3, 0, 1, 2, 4, 5)
    return out.reshape(OUT_LOCAL, PACKED, 2, 128).transpose(0, 2, 1, 3).reshape(OUT_LOCAL, 2, PACKED * 128)


def solution(mesh):
    return jax.shard_map(
        shards,
        mesh=mesh,
        in_specs=(P("band", None, "pw"), P(None, "pw"), P("pw"), P("pw", None), P()),
        out_specs=P("band", None, "pw"),
        check_vma=False,
    )
```

```python
import math

import jax
import jax.numpy as jnp
import numpy as np
from jax import lax
from jax.experimental import pallas as pl
from jax.experimental.pallas import tpu as pltpu
from jax.sharding import PartitionSpec as P
import ml_dtypes

NG = 96
PARTS = 8
PLANES = NG // PARTS
GRID_ROWS = PLANES * NG
GROUPS = 3
SENT = 72
GROUP_ROWS = PARTS * SENT
PACKED = 480
CHIPS = 8
CUBE = ((4, (0, 1, 3, 2)), (1, (0, 3, 4, 7)), (3, (0, 4, 1, 5)))
PIECES = len(CUBE)
PARTED = 4
CHUNK = 2 * PACKED // PIECES // PARTED
HALF = CHUNK // 2
BANDS = 16
OUT_LOCAL = 4
GUARD = 512
BLOCK = 96
FLAG = 1 << 20
MESH = pl.DeviceIdType.MESH
VMEM_SPEC = pl.BlockSpec(memory_space=pltpu.VMEM)
SMEM_SPEC = pl.BlockSpec(memory_space=pltpu.SMEM)
HBM_SPEC = pl.BlockSpec(memory_space=pltpu.HBM)
VMEM_BYTES = 60 * 1024 * 1024


def split_table(table):
    high = table.astype(ml_dtypes.bfloat16)
    low = (table - high.astype(np.float64)).astype(ml_dtypes.bfloat16)
    return np.stack([high, low])


def stacked_table(direction, rows, columns):
    row_part, row_at = np.array(rows).T
    column_part, column_at = np.array(columns).T
    angles = 2.0 * math.pi / NG * (np.outer(row_at, column_at) % NG)
    cosines = np.cos(angles) / math.sqrt(NG)
    sines = direction * np.sin(angles) / math.sqrt(NG)
    same = row_part[:, None] == column_part[None, :]
    signs = np.where(row_part == 0, -1.0, 1.0)[:, None]
    return np.where(same, cosines, signs * sines)


def orders():
    natural = [(p, n) for p in range(2) for n in range(NG)]
    sent_y = [(p, PLANES * d + b) for p in range(2) for b in range(PLANES) for d in range(PARTS)]
    got_x = [
        (p, PLANES * s + 4 * g + t)
        for t in range(4) for g in range(GROUPS) for s in range(PARTS) for p in range(2)
    ]
    back_x = [
        (p, PLANES * e + 4 * g + t)
        for t in range(4) for e in range(PARTS) for g in range(GROUPS) for p in range(2)
    ]
    fin_y = [
        (p, PLANES * s + 4 * h + b)
        for p in range(2) for b in range(4) for h in range(GROUPS) for s in range(PARTS)
    ]
    return natural, sent_y, got_x, back_x, fin_y


def left_tables():
    natural, sent_y, got_x, back_x, fin_y = orders()
    return np.stack([
        split_table(stacked_table(1.0, sent_y, natural)),
        split_table(stacked_table(1.0, natural, got_x)),
        split_table(stacked_table(-1.0, back_x, natural)),
        split_table(stacked_table(-1.0, natural, fin_y)),
    ])


def right_tables():
    natural = orders()[0]
    stack = []
    for direction in (1.0, -1.0):
        table = stacked_table(direction, natural, natural).T
        wide = np.zeros((256, 256))
        for p in range(2):
            for q in range(2):
                wide[128 * p : 128 * p + NG, 128 * q : 128 * q + NG] = table[
                    NG * p : NG * p + NG, NG * q : NG * q + NG
                ]
        stack.append(split_table(wide))
    return np.stack(stack)


def split(value):
    high = value.astype(jnp.bfloat16)
    return high, (value - high.astype(jnp.float32)).astype(jnp.bfloat16)


def dot(a, b):
    return jnp.dot(a, b, preferred_element_type=jnp.float32)


def left_transform(table_ref, which, field):
    high, low = split(field)
    return (
        dot(table_ref[which, 0], high) + dot(table_ref[which, 0], low) + dot(table_ref[which, 1], high)
    )


def right_transform(table_ref, which, field):
    high, low = split(field)
    return (
        dot(high, table_ref[which, 0]) + dot(low, table_ref[which, 0]) + dot(high, table_ref[which, 1])
    )


def cell_of(index):
    line = ((index.astype(jnp.float32) + 0.5) * (1.0 / NG)).astype(jnp.int32)
    return line, index - NG * line


def along(value, lanes):
    return jnp.take_along_axis(value, lanes, axis=1, mode="promise_in_bounds")


def pack_fourth(lane, base, fourth, t):
    return jnp.where(lane < NG, base, pltpu.roll(fourth, NG - 32 * t, 1))


def unpack_fourth(lane, first, second, third):
    return jnp.where(
        lane < 32,
        pltpu.roll(first, 32, 1),
        jnp.where(lane < 64, pltpu.roll(second, 64, 1), pltpu.roll(third, 96, 1)),
    )


def spread(index_ref, wave_ref, real_ref, imag_ref, leave_ref, vr, vi, gap, ready):
    first_line = lax.axis_index("pw") * GRID_ROWS
    lane = lax.broadcasted_iota(jnp.int32, (BLOCK, 128), 1)
    rows = lax.broadcasted_iota(jnp.int32, (BLOCK, 128), 0)
    gap[...] = jnp.zeros_like(gap)
    for ref in (vr, vi):
        ref[pl.ds(0, GUARD), :] = jnp.zeros((GUARD, 128), jnp.float32)
        ref[pl.ds(GUARD + PACKED, GRID_ROWS - PACKED), :] = jnp.zeros((GRID_ROWS - PACKED, 128), jnp.float32)
    ready()
    for step in range(PACKED // BLOCK):
        base = step * BLOCK
        line, z = cell_of(index_ref[pl.ds(base, BLOCK), :])
        position = (rows + base) * 128 + lane
        at = pl.ds(GUARD + base, BLOCK)
        gap[at, :] = ((line - first_line) * 128 + z - position) | FLAG
        vr[at, :] = wave_ref[pl.ds(2 * base, BLOCK, stride=2), :]
        vi[at, :] = wave_ref[pl.ds(2 * base + 1, BLOCK, stride=2), :]

    for bit in range(16, 6, -1):
        shift = 1 << bit
        reach = min(PACKED + sum(1 << k for k in range(bit, 17)) // 128 + 1, GRID_ROWS)
        for step in reversed(range(GRID_ROWS // BLOCK)):
            base = step * BLOCK
            leave_at = pl.ds(base, BLOCK)
            if base >= reach:
                if bit == 16:
                    leave_ref[leave_at, :] = jnp.zeros((BLOCK, 128), jnp.int32)
                continue
            here = pl.ds(GUARD + base, BLOCK)
            there = pl.ds(GUARD + base - shift // 128, BLOCK)
            own = [ref[here, :] for ref in (gap, vr, vi)]
            other = [ref[there, :] for ref in (gap, vr, vi)]
            arrives = (other[0] & shift) != 0
            leaves = own[0] & shift
            held = jnp.where(arrives, other[0], jnp.where(leaves != 0, 0, own[0]))
            leaves = leaves if bit == 16 else leave_ref[leave_at, :] | leaves
            leave_ref[leave_at, :] = leaves if bit > 7 else leaves | (held & 127)
            gap[here, :] = held
            for k, ref in ((1, vr), (2, vi)):
                ref[here, :] = jnp.where(arrives, other[k], own[k])

    for bit in range(6, -1, -1):
        shift = 1 << bit
        stay = lane < 128 - shift
        for step in reversed(range(GRID_ROWS // BLOCK)):
            here = pl.ds(GUARD + step * BLOCK, BLOCK)
            before = pl.ds(GUARD + step * BLOCK - 1, BLOCK)
            own = gap[here, :]
            other = pltpu.roll(jnp.where(stay, own, gap[before, :]), shift, 1)
            held = jnp.where((other & shift) != 0, other, jnp.where((own & shift) != 0, 0, own))
            if bit:
                gap[here, :] = held
                continue
            moved = held & 127
            source = (lane - moved) & 127
            filled = (held & FLAG) != 0
            at = pl.ds(step * BLOCK, BLOCK)
            for ref, target in ((vr, real_ref), (vi, imag_ref)):
                value = jnp.where(lane >= moved, along(ref[here, :], source), along(ref[before, :], source))
                target[at, :] = jnp.where(filled, value, 0.0)


def fields(
    real_ref, imag_ref, rotation_ref, out_real, out_imag, rotations,
    potential_ref, left_ref, right_ref, send, got, back, fin,
    send_sem, recv_sem, own_sem, small_send, small_recv, small_own, enter, tables_ready, potential_ready,
):
    me = lax.axis_index("pw")
    peers = [lax.rem(me + turn, PARTS) for turn in range(PARTS)]
    def start_group(phase, group, source, target):
        copies = []
        for turn, peer in enumerate(peers):
            from_rows = pl.ds(pl.multiple_of(group * GROUP_ROWS + peer * SENT, SENT), SENT)
            to_rows = pl.ds(pl.multiple_of(group * GROUP_ROWS + me * SENT, SENT), SENT)
            if turn:
                copy = pltpu.make_async_remote_copy(
                    src_ref=source.at[from_rows, :],
                    dst_ref=target.at[to_rows, :],
                    send_sem=send_sem.at[phase, group, turn],
                    recv_sem=recv_sem.at[phase, group, turn],
                    device_id={"pw": peer},
                    device_id_type=MESH,
                )
            else:
                copy = pltpu.make_async_copy(
                    source.at[from_rows, :], target.at[to_rows, :], own_sem.at[phase, group]
                )
            copy.start()
            copies.append(copy)
        return copies

    tables_ready()
    lane = lax.broadcasted_iota(jnp.int32, (2 * NG, 128), 1)
    first = []
    for g in range(GROUPS):
        planes = []
        for pair in range(2):
            stacked = []
            for t in (2 * pair, 2 * pair + 1):
                at = pl.ds((4 * g + t) * NG, NG)
                field = jnp.concatenate([real_ref[at, :], imag_ref[at, :]], axis=1).astype(jnp.bfloat16)
                field = dot(field, right_ref[0, 0]) + dot(field, right_ref[0, 1])
                stacked.append(jnp.concatenate([field[:, :128], field[:, 128:]], axis=0))
            both = left_transform(left_ref, 0, jnp.concatenate(stacked, axis=1))
            planes += [both[:, :128], both[:, 128:]]
        for t in range(3):
            packed = pack_fourth(lane, planes[t], planes[3], t)
            for p in range(2):
                for b in range(PLANES):
                    row = (p * PLANES + b) * PARTS
                    at = pl.ds(g * GROUP_ROWS + (p * 3 + t) * PLANES + b, PARTS, stride=SENT)
                    send[at, :] = packed[row : row + PARTS]
        if g == 0:
            enter()
        first += start_group(0, g, send, got)

    small = []
    for turn, peer in enumerate(peers):
        if turn:
            copy = pltpu.make_async_remote_copy(
                src_ref=rotation_ref,
                dst_ref=rotations.at[me],
                send_sem=small_send.at[turn],
                recv_sem=small_recv.at[turn],
                device_id={"pw": peer},
                device_id_type=MESH,
            )
        else:
            copy = pltpu.make_async_copy(rotation_ref, rotations.at[me], small_own.at[0])
        copy.start()
        small.append(copy)

    potential_ready()
    for copy in first:
        copy.wait()
    lane48 = lax.broadcasted_iota(jnp.int32, (48, 128), 1)
    second = []
    for group in range(GROUPS):
        for pair in range(2):
            stacked, local = [], []
            for b in (4 * group + 2 * pair, 4 * group + 2 * pair + 1):
                planes = [got[pl.ds(t * PLANES + b, 48, stride=36), :] for t in range(3)]
                planes.append(unpack_fourth(lane48, *planes))
                stacked.append(jnp.concatenate(planes, axis=0))
                offset = b * NG % 128
                start = b * NG - offset
                if offset + NG > 128:
                    part = pltpu.roll(potential_ref[:, start : start + 256], 256 - offset, 1)[:, :128]
                else:
                    part = potential_ref[:, start : start + 128]
                    if offset:
                        part = pltpu.roll(part, 128 - offset, 1)
                local.append(part)
            local = jnp.concatenate(local, axis=1)
            field = left_transform(left_ref, 1, jnp.concatenate(stacked, axis=1))
            field = jnp.concatenate([local, local], axis=0) * field
            field = left_transform(left_ref, 2, field)
            for column in range(2):
                planes = [field[48 * t : 48 * t + 48, 128 * column : 128 * column + 128] for t in range(4)]
                for t in range(3):
                    at = pl.ds(group * GROUP_ROWS + t * 4 + 2 * pair + column, 48, stride=PLANES)
                    back[at, :] = pack_fourth(lane48, planes[t], planes[3], t)
        second += start_group(1, group, back, fin)
    for copy in second + small:
        copy.wait()
    lane96 = lax.broadcasted_iota(jnp.int32, (NG, 128), 1)
    for g in range(GROUPS):
        parts = []
        for p in range(2):
            planes = [
                jnp.concatenate(
                    [
                        fin[pl.ds(g * 24 + p * PLANES + t * 4 + b, 24, stride=SENT), :]
                        for b in range(4)
                    ],
                    axis=0,
                )
                for t in range(3)
            ]
            planes.append(unpack_fourth(lane96, *planes))
            parts.append(planes)
        for pair in range(2):
            stacked = [
                jnp.concatenate([parts[0][t], parts[1][t]], axis=0) for t in (2 * pair, 2 * pair + 1)
            ]
            both = left_transform(left_ref, 3, jnp.concatenate(stacked, axis=1))
            for column in range(2):
                plane = both[:, 128 * column : 128 * column + 128]
                field = jnp.concatenate([plane[:NG], plane[NG:]], axis=1)
                field = right_transform(right_ref, 1, field)
                at = pl.ds((4 * g + 2 * pair + column) * NG, NG)
                out_real[at, :] = field[:, :128]
                out_imag[at, :] = field[:, 128:]


def pick(leave_ref, wave_ref, index_ref, applied_ref, vr, vi):
    lane = lax.broadcasted_iota(jnp.int32, (BLOCK, 128), 1)
    for step in range(GRID_ROWS // BLOCK):
        here = pl.ds(step * BLOCK, BLOCK)
        after = pl.ds(step * BLOCK + 1, BLOCK)
        source = lane + (leave_ref[here, :] & 127)
        inside = source < 128
        source = source & 127
        for ref in (vr, vi):
            ref[here, :] = jnp.where(inside, along(ref[here, :], source), along(ref[after, :], source))
    for bit in range(7, 17):
        shift = 1 << bit
        needed = PACKED + sum(1 << k for k in range(bit + 1, 17)) // 128 + 1
        for step in range(GRID_ROWS // BLOCK):
            base = step * BLOCK
            if base >= needed:
                continue
            here = pl.ds(base, BLOCK)
            there = pl.ds(base + shift // 128, BLOCK)
            arrives = (leave_ref[here, :] & shift) != 0
            for ref in (vr, vi):
                ref[here, :] = jnp.where(arrives, ref[there, :], ref[here, :])

    def signed_square(position):
        signed = jnp.where(position < NG // 2, position, position - NG).astype(jnp.float32)
        return signed * signed

    def finish(step):
        base = step * BLOCK
        line, z = cell_of(index_ref[pl.ds(base, BLOCK), :])
        x, y = cell_of(line)
        energy = 2.0 * (signed_square(x) + signed_square(y) + signed_square(z)) / float((NG // 2) ** 2)
        for part, ref in enumerate((vr, vi)):
            at = pl.ds(2 * base + part, BLOCK, stride=2)
            applied_ref[at, :] = energy * wave_ref[at, :] + ref[pl.ds(base, BLOCK), :]

    return finish


def across(chip, mask):
    z, x = chip // 4, chip % 4
    x = (x, x + 1 - 2 * (x % 2), (x + 2) % 4, 3 - x)[mask % 4]
    return (1 - z if mask >= 4 else z) * 4 + x


def part_of(chip, piece):
    z, x = chip // 4, chip % 4
    near, far = (x + x // 2) % 2, x // 2
    return (near + 2 * far, far + 2 * z, near + 2 * z)[piece]


def rotate(
    finish, applied_ref, rotations, order_ref, out_ref, window, mixed,
    first_send, first_recv, relay_send, relay_recv, out_send, out_recv, own_sem,
):
    band = lax.axis_index("band")
    chip, core = band // 2, band % 2
    cores = (core, 1 - core)

    def rows(which, piece, half):
        start = piece * PARTED * CHUNK + part_of(which, piece) * CHUNK + half * HALF
        return pl.ds(pl.multiple_of(start, HALF), HALF)

    def move(source, target, peer, turn, send, recv, own):
        if turn:
            copy = pltpu.make_async_remote_copy(
                src_ref=source,
                dst_ref=target,
                send_sem=send,
                recv_sem=recv,
                device_id={"band": peer},
                device_id_type=MESH,
            )
        else:
            copy = pltpu.make_async_copy(source, target, own)
        copy.start()
        return copy

    relayed, results = [], []
    sent = [[None] * CHIPS for _ in CUBE]
    done = 0
    for piece, (_, masks) in enumerate(CUBE):
        while done * 2 * BLOCK < (piece + 1) * PARTED * CHUNK:
            finish(done)
            done += 1
        for k in reversed(range(PARTED)):
            peer = across(chip, masks[k])
            for c, half in enumerate(cores):
                turn = 2 * k + c
                sent[piece][turn] = move(
                    applied_ref.at[rows(peer, piece, half), :], window.at[piece, 2 * k + core],
                    peer * 2 + half, turn, first_send.at[piece, turn], first_recv.at[piece, turn],
                    own_sem.at[0, piece],
                )

    def relay(piece):
        sent[piece][0].wait()
        for copy in sent[piece][1:]:
            copy.wait_recv()
        relayed.append(move(
            window.at[piece, pl.ds(0, CHIPS)], window.at[piece, pl.ds(CHIPS, CHIPS)],
            across(chip, CUBE[piece][0]) * 2 + core, 1, relay_send.at[piece], relay_recv.at[piece], None,
        ))

    def panels_of(piece):
        shared, masks = CUBE[piece]
        panels = []
        for start in (chip, across(chip, shared)):
            for mask in masks:
                for c in range(2):
                    panel = order_ref[across(start, mask) * 2 + c]
                    panels.append((panel // 2, panel % 2))
        return panels

    def mix(piece, k, c, panels):
        peer = across(chip, CUBE[piece][1][k]) * 2 + cores[c]
        turn = 2 * k + c
        totals = [None] * OUT_LOCAL
        for i in range(BANDS):
            term = window[piece, i]
            for j in range(OUT_LOCAL):
                factor = rotations[panels[i][0], panels[i][1], peer * OUT_LOCAL + j]
                totals[j] = factor * term if i == 0 else totals[j] + factor * term
        for j in range(OUT_LOCAL):
            mixed[piece, turn, j] = totals[j]
        results.append(move(
            mixed.at[piece, turn], out_ref.at[piece, part_of(chip, piece), core],
            peer, turn, out_send.at[piece, turn], out_recv.at[piece, turn], own_sem.at[1, piece],
        ))

    for piece in range(PIECES):
        relay(piece)
    panels = [panels_of(piece) for piece in range(PIECES)]
    for k in reversed(range(PARTED)):
        for c in (1, 0):
            for piece in range(PIECES):
                if k == PARTED - 1 and c:
                    relayed[piece].wait_recv()
                mix(piece, k, c, panels[piece])
    for copies in sent:
        for copy in copies[1:]:
            copy.wait_send()
    for copy in relayed:
        copy.wait_send()
    for copy in results:
        copy.wait()


def whole_kernel(
    index_hbm, wave_hbm, potential_hbm, rotation_ref, order_ref, left_hbm, right_hbm,
    out_ref,
    index_ref, narrow_ref, wave_ref, potential_ref, left_ref, right_ref,
    real_ref, imag_ref, leave_ref, vr, vi, gap, send, got, back, fin, rotations, factors, applied_ref, window, mixed,
    load_sem, send_sem, recv_sem, own_sem, small_send, small_recv, small_own,
    first_send, first_recv, relay_send, relay_recv, out_send, out_recv, band_own,
):
    loads = [
        pltpu.make_async_copy(source, target, load_sem.at[k])
        for k, (source, target) in enumerate((
            (index_hbm, index_ref), (wave_hbm, narrow_ref), (right_hbm, right_ref),
            (left_hbm, left_ref), (potential_hbm, potential_ref),
        ))
    ]
    for load in loads:
        load.start()
    me, band = lax.axis_index("pw"), lax.axis_index("band")
    barrier = pltpu.get_barrier_semaphore()
    for turn in range(1, PARTS):
        pl.semaphore_signal(
            barrier, inc=1, device_id={"pw": lax.rem(me + turn, PARTS)}, device_id_type=MESH
        )
    for turn in range(1, BANDS):
        peer = lax.rem(band + turn, BANDS)
        pl.semaphore_signal(barrier, inc=1, device_id={"band": peer}, device_id_type=MESH)

    def ready(*which):
        def wait():
            for k in which:
                loads[k].wait()

        return wait

    def inputs_ready():
        ready(0, 1)()
        wave_ref[...] = narrow_ref[...].astype(jnp.float32)

    spread(index_ref, wave_ref, real_ref, imag_ref, leave_ref, vr, vi, gap, inputs_ready)
    fields(
        real_ref, imag_ref, rotation_ref, vr, vi, rotations,
        potential_ref, left_ref, right_ref, send, got, back, fin,
        send_sem, recv_sem, own_sem, small_send, small_recv, small_own,
        lambda: pl.semaphore_wait(barrier, PARTS - 1 + BANDS - 1), ready(2, 3), ready(4),
    )
    to_scalars = pltpu.make_async_copy(rotations, factors, small_own.at[1])
    to_scalars.start()
    finish = pick(leave_ref, wave_ref, index_ref, applied_ref, vr, vi)
    to_scalars.wait()
    rotate(
        finish, applied_ref, factors, order_ref, out_ref, window, mixed,
        first_send, first_recv, relay_send, relay_recv, out_send, out_recv, band_own,
    )


def shards(wave_coeffs, potential, sphere_index, rotation, panel_order):
    f32 = jnp.float32
    bf16 = jnp.bfloat16
    values = wave_coeffs.reshape(2, PACKED, 128).transpose(1, 0, 2).reshape(2 * PACKED, 128)
    index = sphere_index.reshape(PACKED, 128)
    left, right = left_tables(), right_tables()
    exchange_buffer = pltpu.VMEM((GROUPS * GROUP_ROWS, 128), f32)
    grid_buffer = pltpu.VMEM((GRID_ROWS, 128), f32)
    dma = pltpu.SemaphoreType.DMA

    def wide(kind):
        return pltpu.VMEM((GUARD + GRID_ROWS, 128), kind)

    out = pl.pallas_call(
        whole_kernel,
        out_shape=jax.ShapeDtypeStruct((PIECES, PARTED, 2, OUT_LOCAL, HALF, 128), f32),
        in_specs=[HBM_SPEC, HBM_SPEC, HBM_SPEC, VMEM_SPEC, SMEM_SPEC, HBM_SPEC, HBM_SPEC],
        out_specs=HBM_SPEC,
        scratch_shapes=[
            pltpu.VMEM((PACKED, 128), jnp.int32),
            pltpu.VMEM((2 * PACKED, 128), bf16),
            pltpu.VMEM((2 * PACKED, 128), f32),
            pltpu.VMEM(potential.shape, f32),
            pltpu.VMEM(left.shape, bf16),
            pltpu.VMEM(right.shape, bf16),
            grid_buffer,
            grid_buffer,
            pltpu.VMEM((GRID_ROWS, 128), jnp.int32),
            wide(f32),
            wide(f32),
            wide(jnp.int32),
        ]
        + [exchange_buffer] * 4
        + [
            pltpu.VMEM((PARTS, 2, 64), f32),
            pltpu.SMEM((PARTS, 2, 64), f32),
            pltpu.VMEM((2 * PACKED, 128), f32),
            pltpu.VMEM((PIECES, BANDS, HALF, 128), f32),
            pltpu.VMEM((PIECES, CHIPS, OUT_LOCAL, HALF, 128), f32),
            dma((5,)),
            dma((2, GROUPS, PARTS)),
            dma((2, GROUPS, PARTS)),
            dma((2, GROUPS)),
            dma((PARTS,)),
            dma((PARTS,)),
            dma((2,)),
        ]
        + [dma((PIECES, CHIPS))] * 2
        + [dma((PIECES,))] * 2
        + [dma((PIECES, CHIPS))] * 2
        + [dma((2, PIECES))],
        compiler_params=pltpu.CompilerParams(
            vmem_limit_bytes=VMEM_BYTES, collective_id=0, has_side_effects=True
        ),
        name="whole",
    )(index, values, potential, rotation, panel_order, jnp.asarray(left), jnp.asarray(right))
    out = out.transpose(3, 0, 1, 2, 4, 5)
    return out.reshape(OUT_LOCAL, PACKED, 2, 128).transpose(0, 2, 1, 3).reshape(OUT_LOCAL, 2, PACKED * 128)


def solution(mesh):
    return jax.shard_map(
        shards,
        mesh=mesh,
        in_specs=(P("band", None, "pw"), P(None, "pw"), P("pw"), P("pw", None), P()),
        out_specs=P("band", None, "pw"),
        check_vma=False,
    )
```

```python
import math

import jax
import jax.numpy as jnp
import numpy as np
from jax import lax
from jax.experimental import pallas as pl
from jax.experimental.pallas import tpu as pltpu
from jax.sharding import PartitionSpec as P
import ml_dtypes

NG = 96
PARTS = 8
PLANES = NG // PARTS
GRID_ROWS = PLANES * NG
GROUPS = 3
SENT = 72
GROUP_ROWS = PARTS * SENT
PACKED = 480
CHIPS = 8
CUBE = ((4, (0, 1, 3, 2)), (1, (0, 3, 4, 7)), (3, (0, 4, 1, 5)))
PIECES = len(CUBE)
PARTED = 4
CHUNK = 2 * PACKED // PIECES // PARTED
HALF = CHUNK // 2
BANDS = 16
OUT_LOCAL = 4
GUARD = 512
BLOCK = 96
FLAG = 1 << 20
MESH = pl.DeviceIdType.MESH
VMEM_SPEC = pl.BlockSpec(memory_space=pltpu.VMEM)
SMEM_SPEC = pl.BlockSpec(memory_space=pltpu.SMEM)
HBM_SPEC = pl.BlockSpec(memory_space=pltpu.HBM)
VMEM_BYTES = 60 * 1024 * 1024


def split_table(table):
    high = table.astype(ml_dtypes.bfloat16)
    low = (table - high.astype(np.float64)).astype(ml_dtypes.bfloat16)
    return np.stack([high, low])


def stacked_table(direction, rows, columns):
    row_part, row_at = np.array(rows).T
    column_part, column_at = np.array(columns).T
    angles = 2.0 * math.pi / NG * (np.outer(row_at, column_at) % NG)
    cosines = np.cos(angles) / math.sqrt(NG)
    sines = direction * np.sin(angles) / math.sqrt(NG)
    same = row_part[:, None] == column_part[None, :]
    signs = np.where(row_part == 0, -1.0, 1.0)[:, None]
    return np.where(same, cosines, signs * sines)


def orders():
    natural = [(p, n) for p in range(2) for n in range(NG)]
    sent_y = [(p, PLANES * d + b) for p in range(2) for b in range(PLANES) for d in range(PARTS)]
    got_x = [
        (p, PLANES * s + 4 * g + t)
        for t in range(4) for g in range(GROUPS) for s in range(PARTS) for p in range(2)
    ]
    back_x = [
        (p, PLANES * e + 4 * g + t)
        for t in range(4) for e in range(PARTS) for g in range(GROUPS) for p in range(2)
    ]
    fin_y = [
        (p, PLANES * s + 4 * h + b)
        for p in range(2) for b in range(4) for h in range(GROUPS) for s in range(PARTS)
    ]
    return natural, sent_y, got_x, back_x, fin_y


def left_tables():
    natural, sent_y, got_x, back_x, fin_y = orders()
    return np.stack([
        split_table(stacked_table(1.0, sent_y, natural)),
        split_table(stacked_table(1.0, natural, got_x)),
        split_table(stacked_table(-1.0, back_x, natural)),
        split_table(stacked_table(-1.0, natural, fin_y)),
    ])


def right_tables():
    natural = orders()[0]
    stack = []
    for direction in (1.0, -1.0):
        table = stacked_table(direction, natural, natural).T
        wide = np.zeros((256, 256))
        for p in range(2):
            for q in range(2):
                wide[128 * p : 128 * p + NG, 128 * q : 128 * q + NG] = table[
                    NG * p : NG * p + NG, NG * q : NG * q + NG
                ]
        stack.append(split_table(wide))
    return np.stack(stack)


def split(value):
    high = value.astype(jnp.bfloat16)
    return high, (value - high.astype(jnp.float32)).astype(jnp.bfloat16)


def dot(a, b):
    return jnp.dot(a, b, preferred_element_type=jnp.float32)


def left_transform(table_ref, which, field):
    high, low = split(field)
    return (
        dot(table_ref[which, 0], high) + dot(table_ref[which, 0], low) + dot(table_ref[which, 1], high)
    )


def right_transform(table_ref, which, field):
    high, low = split(field)
    return (
        dot(high, table_ref[which, 0]) + dot(low, table_ref[which, 0]) + dot(high, table_ref[which, 1])
    )


def cell_of(index):
    line = ((index.astype(jnp.float32) + 0.5) * (1.0 / NG)).astype(jnp.int32)
    return line, index - NG * line


def along(value, lanes):
    return jnp.take_along_axis(value, lanes, axis=1, mode="promise_in_bounds")


def pack_fourth(lane, base, fourth, t):
    return jnp.where(lane < NG, base, pltpu.roll(fourth, NG - 32 * t, 1))


def unpack_fourth(lane, first, second, third):
    return jnp.where(
        lane < 32,
        pltpu.roll(first, 32, 1),
        jnp.where(lane < 64, pltpu.roll(second, 64, 1), pltpu.roll(third, 96, 1)),
    )


def spread(index_ref, wave_ref, real_ref, imag_ref, leave_ref, vr, vi, gap, ready):
    first_line = lax.axis_index("pw") * GRID_ROWS
    lane = lax.broadcasted_iota(jnp.int32, (BLOCK, 128), 1)
    rows = lax.broadcasted_iota(jnp.int32, (BLOCK, 128), 0)
    gap[...] = jnp.zeros_like(gap)
    for ref in (vr, vi):
        ref[pl.ds(0, GUARD), :] = jnp.zeros((GUARD, 128), jnp.float32)
        ref[pl.ds(GUARD + PACKED, GRID_ROWS - PACKED), :] = jnp.zeros((GRID_ROWS - PACKED, 128), jnp.float32)
    ready()
    for step in range(PACKED // BLOCK):
        base = step * BLOCK
        line, z = cell_of(index_ref[pl.ds(base, BLOCK), :])
        position = (rows + base) * 128 + lane
        at = pl.ds(GUARD + base, BLOCK)
        gap[at, :] = ((line - first_line) * 128 + z - position) | FLAG
        vr[at, :] = wave_ref[pl.ds(2 * base, BLOCK, stride=2), :]
        vi[at, :] = wave_ref[pl.ds(2 * base + 1, BLOCK, stride=2), :]

    for bit in range(16, 6, -1):
        shift = 1 << bit
        reach = min(PACKED + sum(1 << k for k in range(bit, 17)) // 128 + 1, GRID_ROWS)
        for step in reversed(range(GRID_ROWS // BLOCK)):
            base = step * BLOCK
            leave_at = pl.ds(base, BLOCK)
            if base >= reach:
                if bit == 16:
                    leave_ref[leave_at, :] = jnp.zeros((BLOCK, 128), jnp.int32)
                continue
            here = pl.ds(GUARD + base, BLOCK)
            there = pl.ds(GUARD + base - shift // 128, BLOCK)
            own = [ref[here, :] for ref in (gap, vr, vi)]
            other = [ref[there, :] for ref in (gap, vr, vi)]
            arrives = (other[0] & shift) != 0
            leaves = own[0] & shift
            held = jnp.where(arrives, other[0], jnp.where(leaves != 0, 0, own[0]))
            leaves = leaves if bit == 16 else leave_ref[leave_at, :] | leaves
            leave_ref[leave_at, :] = leaves if bit > 7 else leaves | (held & 127)
            gap[here, :] = held
            for k, ref in ((1, vr), (2, vi)):
                ref[here, :] = jnp.where(arrives, other[k], own[k])

    for bit in range(6, -1, -1):
        shift = 1 << bit
        stay = lane < 128 - shift
        for step in reversed(range(GRID_ROWS // BLOCK)):
            here = pl.ds(GUARD + step * BLOCK, BLOCK)
            before = pl.ds(GUARD + step * BLOCK - 1, BLOCK)
            own = gap[here, :]
            other = pltpu.roll(jnp.where(stay, own, gap[before, :]), shift, 1)
            held = jnp.where((other & shift) != 0, other, jnp.where((own & shift) != 0, 0, own))
            if bit:
                gap[here, :] = held
                continue
            moved = held & 127
            source = (lane - moved) & 127
            filled = (held & FLAG) != 0
            at = pl.ds(step * BLOCK, BLOCK)
            for ref, target in ((vr, real_ref), (vi, imag_ref)):
                value = jnp.where(lane >= moved, along(ref[here, :], source), along(ref[before, :], source))
                target[at, :] = jnp.where(filled, value, 0.0)


def fields(
    real_ref, imag_ref, rotation_ref, out_real, out_imag, rotations,
    potential_ref, left_ref, right_ref, send, got, back, fin,
    send_sem, recv_sem, own_sem, small_send, small_recv, small_own, enter, tables_ready, potential_ready,
):
    me = lax.axis_index("pw")
    peers = [lax.rem(me + turn, PARTS) for turn in range(PARTS)]
    def start_group(phase, group, source, target):
        copies = []
        for turn, peer in enumerate(peers):
            from_rows = pl.ds(pl.multiple_of(group * GROUP_ROWS + peer * SENT, SENT), SENT)
            to_rows = pl.ds(pl.multiple_of(group * GROUP_ROWS + me * SENT, SENT), SENT)
            if turn:
                copy = pltpu.make_async_remote_copy(
                    src_ref=source.at[from_rows, :],
                    dst_ref=target.at[to_rows, :],
                    send_sem=send_sem.at[phase, group, turn],
                    recv_sem=recv_sem.at[phase, group, turn],
                    device_id={"pw": peer},
                    device_id_type=MESH,
                )
            else:
                copy = pltpu.make_async_copy(
                    source.at[from_rows, :], target.at[to_rows, :], own_sem.at[phase, group]
                )
            copy.start()
            copies.append(copy)
        return copies

    tables_ready()
    lane = lax.broadcasted_iota(jnp.int32, (2 * NG, 128), 1)
    first = []
    for g in range(GROUPS):
        planes = []
        for pair in range(2):
            stacked = []
            for t in (2 * pair, 2 * pair + 1):
                at = pl.ds((4 * g + t) * NG, NG)
                field = jnp.concatenate([real_ref[at, :], imag_ref[at, :]], axis=1).astype(jnp.bfloat16)
                field = dot(field, right_ref[0, 0]) + dot(field, right_ref[0, 1])
                stacked.append(jnp.concatenate([field[:, :128], field[:, 128:]], axis=0))
            both = left_transform(left_ref, 0, jnp.concatenate(stacked, axis=1))
            planes += [both[:, :128], both[:, 128:]]
        for t in range(3):
            packed = pack_fourth(lane, planes[t], planes[3], t)
            for p in range(2):
                for b in range(PLANES):
                    row = (p * PLANES + b) * PARTS
                    at = pl.ds(g * GROUP_ROWS + (p * 3 + t) * PLANES + b, PARTS, stride=SENT)
                    send[at, :] = packed[row : row + PARTS]
        if g == 0:
            enter()
        first += start_group(0, g, send, got)

    small = []
    for turn, peer in enumerate(peers):
        if turn:
            copy = pltpu.make_async_remote_copy(
                src_ref=rotation_ref,
                dst_ref=rotations.at[me],
                send_sem=small_send.at[turn],
                recv_sem=small_recv.at[turn],
                device_id={"pw": peer},
                device_id_type=MESH,
            )
        else:
            copy = pltpu.make_async_copy(rotation_ref, rotations.at[me], small_own.at[0])
        copy.start()
        small.append(copy)

    potential_ready()
    for copy in first:
        copy.wait()
    lane48 = lax.broadcasted_iota(jnp.int32, (48, 128), 1)
    second = []
    for group in range(GROUPS):
        for pair in range(2):
            stacked, local = [], []
            for b in (4 * group + 2 * pair, 4 * group + 2 * pair + 1):
                planes = [got[pl.ds(t * PLANES + b, 48, stride=36), :] for t in range(3)]
                planes.append(unpack_fourth(lane48, *planes))
                stacked.append(jnp.concatenate(planes, axis=0))
                offset = b * NG % 128
                start = b * NG - offset
                if offset + NG > 128:
                    part = pltpu.roll(potential_ref[:, start : start + 256], 256 - offset, 1)[:, :128]
                else:
                    part = potential_ref[:, start : start + 128]
                    if offset:
                        part = pltpu.roll(part, 128 - offset, 1)
                local.append(part)
            local = jnp.concatenate(local, axis=1)
            field = left_transform(left_ref, 1, jnp.concatenate(stacked, axis=1))
            field = jnp.concatenate([local, local], axis=0) * field
            field = left_transform(left_ref, 2, field)
            for column in range(2):
                planes = [field[48 * t : 48 * t + 48, 128 * column : 128 * column + 128] for t in range(4)]
                for t in range(3):
                    at = pl.ds(group * GROUP_ROWS + t * 4 + 2 * pair + column, 48, stride=PLANES)
                    back[at, :] = pack_fourth(lane48, planes[t], planes[3], t)
        second += start_group(1, group, back, fin)
    for copy in second + small:
        copy.wait()
    lane96 = lax.broadcasted_iota(jnp.int32, (NG, 128), 1)
    for g in range(GROUPS):
        parts = []
        for p in range(2):
            planes = [
                jnp.concatenate(
                    [
                        fin[pl.ds(g * 24 + p * PLANES + t * 4 + b, 24, stride=SENT), :]
                        for b in range(4)
                    ],
                    axis=0,
                )
                for t in range(3)
            ]
            planes.append(unpack_fourth(lane96, *planes))
            parts.append(planes)
        for pair in range(2):
            stacked = [
                jnp.concatenate([parts[0][t], parts[1][t]], axis=0) for t in (2 * pair, 2 * pair + 1)
            ]
            both = left_transform(left_ref, 3, jnp.concatenate(stacked, axis=1))
            for column in range(2):
                plane = both[:, 128 * column : 128 * column + 128]
                field = jnp.concatenate([plane[:NG], plane[NG:]], axis=1)
                field = right_transform(right_ref, 1, field)
                at = pl.ds((4 * g + 2 * pair + column) * NG, NG)
                out_real[at, :] = field[:, :128]
                out_imag[at, :] = field[:, 128:]


def pick(leave_ref, wave_ref, index_ref, applied_ref, vr, vi):
    lane = lax.broadcasted_iota(jnp.int32, (BLOCK, 128), 1)
    for step in range(GRID_ROWS // BLOCK):
        here = pl.ds(step * BLOCK, BLOCK)
        after = pl.ds(step * BLOCK + 1, BLOCK)
        source = lane + (leave_ref[here, :] & 127)
        inside = source < 128
        source = source & 127
        for ref in (vr, vi):
            ref[here, :] = jnp.where(inside, along(ref[here, :], source), along(ref[after, :], source))
    for bit in range(7, 17):
        shift = 1 << bit
        needed = PACKED + sum(1 << k for k in range(bit + 1, 17)) // 128 + 1
        for step in range(GRID_ROWS // BLOCK):
            base = step * BLOCK
            if base >= needed:
                continue
            here = pl.ds(base, BLOCK)
            there = pl.ds(base + shift // 128, BLOCK)
            arrives = (leave_ref[here, :] & shift) != 0
            for ref in (vr, vi):
                ref[here, :] = jnp.where(arrives, ref[there, :], ref[here, :])

    def signed_square(position):
        signed = jnp.where(position < NG // 2, position, position - NG).astype(jnp.float32)
        return signed * signed

    def finish(step):
        base = step * BLOCK
        line, z = cell_of(index_ref[pl.ds(base, BLOCK), :])
        x, y = cell_of(line)
        energy = 2.0 * (signed_square(x) + signed_square(y) + signed_square(z)) / float((NG // 2) ** 2)
        for part, ref in enumerate((vr, vi)):
            at = pl.ds(2 * base + part, BLOCK, stride=2)
            applied_ref[at, :] = energy * wave_ref[at, :] + ref[pl.ds(base, BLOCK), :]

    return finish


def across(chip, mask):
    z, x = chip // 4, chip % 4
    x = (x, x + 1 - 2 * (x % 2), (x + 2) % 4, 3 - x)[mask % 4]
    return (1 - z if mask >= 4 else z) * 4 + x


def part_of(chip, piece):
    z, x = chip // 4, chip % 4
    near, far = (x + x // 2) % 2, x // 2
    return (near + 2 * far, far + 2 * z, near + 2 * z)[piece]


def rotate(
    finish, applied_ref, rotations, order_ref, out_ref, window, mixed,
    first_send, first_recv, relay_send, relay_recv, out_send, out_recv, own_sem,
):
    band = lax.axis_index("band")
    chip, core = band // 2, band % 2
    cores = (core, 1 - core)

    def rows(which, piece, half):
        start = piece * PARTED * CHUNK + part_of(which, piece) * CHUNK + half * HALF
        return pl.ds(pl.multiple_of(start, HALF), HALF)

    def move(source, target, peer, turn, send, recv, own):
        if turn:
            copy = pltpu.make_async_remote_copy(
                src_ref=source,
                dst_ref=target,
                send_sem=send,
                recv_sem=recv,
                device_id={"band": peer},
                device_id_type=MESH,
            )
        else:
            copy = pltpu.make_async_copy(source, target, own)
        copy.start()
        return copy

    relayed, results = [], []
    sent = [[None] * CHIPS for _ in CUBE]
    done = 0
    for piece, (_, masks) in enumerate(CUBE):
        while done * 2 * BLOCK < (piece + 1) * PARTED * CHUNK:
            finish(done)
            done += 1
        for c, half in ((1, cores[1]), (0, cores[0])):
            for k in reversed(range(PARTED)):
                peer = across(chip, masks[k])
                turn = 2 * k + c
                sent[piece][turn] = move(
                    applied_ref.at[rows(peer, piece, half), :], window.at[piece, 2 * k + core],
                    peer * 2 + half, turn, first_send.at[piece, turn], first_recv.at[piece, turn],
                    own_sem.at[0, piece],
                )

    def relay(piece):
        sent[piece][0].wait()
        for copy in sent[piece][1:]:
            copy.wait_recv()
        relayed.append(move(
            window.at[piece, pl.ds(0, CHIPS)], window.at[piece, pl.ds(CHIPS, CHIPS)],
            across(chip, CUBE[piece][0]) * 2 + core, 1, relay_send.at[piece], relay_recv.at[piece], None,
        ))

    def panels_of(piece):
        shared, masks = CUBE[piece]
        panels = []
        for start in (chip, across(chip, shared)):
            for mask in masks:
                for c in range(2):
                    panel = order_ref[across(start, mask) * 2 + c]
                    panels.append((panel // 2, panel % 2))
        return panels

    def mix(piece, k, c, panels):
        peer = across(chip, CUBE[piece][1][k]) * 2 + cores[c]
        turn = 2 * k + c
        totals = [None] * OUT_LOCAL
        for i in range(BANDS):
            term = window[piece, i]
            for j in range(OUT_LOCAL):
                factor = rotations[panels[i][0], panels[i][1], peer * OUT_LOCAL + j]
                totals[j] = factor * term if i == 0 else totals[j] + factor * term
        for j in range(OUT_LOCAL):
            mixed[piece, turn, j] = totals[j]
        results.append(move(
            mixed.at[piece, turn], out_ref.at[piece, part_of(chip, piece), core],
            peer, turn, out_send.at[piece, turn], out_recv.at[piece, turn], own_sem.at[1, piece],
        ))

    for piece in range(PIECES):
        relay(piece)
    panels = [panels_of(piece) for piece in range(PIECES)]
    for k in reversed(range(PARTED)):
        for c in (1, 0):
            for piece in range(PIECES):
                if k == PARTED - 1 and c:
                    relayed[piece].wait_recv()
                mix(piece, k, c, panels[piece])
    for copies in sent:
        for copy in copies[1:]:
            copy.wait_send()
    for copy in relayed:
        copy.wait_send()
    for copy in results:
        copy.wait()


def whole_kernel(
    index_hbm, wave_hbm, potential_hbm, rotation_ref, order_ref, left_hbm, right_hbm,
    out_ref,
    index_ref, narrow_ref, wave_ref, potential_ref, left_ref, right_ref,
    real_ref, imag_ref, leave_ref, vr, vi, gap, send, got, back, fin, rotations, factors, applied_ref, window, mixed,
    load_sem, send_sem, recv_sem, own_sem, small_send, small_recv, small_own,
    first_send, first_recv, relay_send, relay_recv, out_send, out_recv, band_own,
):
    loads = [
        pltpu.make_async_copy(source, target, load_sem.at[k])
        for k, (source, target) in enumerate((
            (index_hbm, index_ref), (wave_hbm, narrow_ref), (right_hbm, right_ref),
            (left_hbm, left_ref), (potential_hbm, potential_ref),
        ))
    ]
    for load in loads:
        load.start()
    me, band = lax.axis_index("pw"), lax.axis_index("band")
    barrier = pltpu.get_barrier_semaphore()
    for turn in range(1, PARTS):
        pl.semaphore_signal(
            barrier, inc=1, device_id={"pw": lax.rem(me + turn, PARTS)}, device_id_type=MESH
        )
    for turn in range(1, BANDS):
        peer = lax.rem(band + turn, BANDS)
        pl.semaphore_signal(barrier, inc=1, device_id={"band": peer}, device_id_type=MESH)

    def ready(*which):
        def wait():
            for k in which:
                loads[k].wait()

        return wait

    def inputs_ready():
        ready(0, 1)()
        wave_ref[...] = narrow_ref[...].astype(jnp.float32)

    spread(index_ref, wave_ref, real_ref, imag_ref, leave_ref, vr, vi, gap, inputs_ready)
    fields(
        real_ref, imag_ref, rotation_ref, vr, vi, rotations,
        potential_ref, left_ref, right_ref, send, got, back, fin,
        send_sem, recv_sem, own_sem, small_send, small_recv, small_own,
        lambda: pl.semaphore_wait(barrier, PARTS - 1 + BANDS - 1), ready(2, 3), ready(4),
    )
    to_scalars = pltpu.make_async_copy(rotations, factors, small_own.at[1])
    to_scalars.start()
    finish = pick(leave_ref, wave_ref, index_ref, applied_ref, vr, vi)
    to_scalars.wait()
    rotate(
        finish, applied_ref, factors, order_ref, out_ref, window, mixed,
        first_send, first_recv, relay_send, relay_recv, out_send, out_recv, band_own,
    )


def shards(wave_coeffs, potential, sphere_index, rotation, panel_order):
    f32 = jnp.float32
    bf16 = jnp.bfloat16
    values = wave_coeffs.reshape(2, PACKED, 128).transpose(1, 0, 2).reshape(2 * PACKED, 128)
    index = sphere_index.reshape(PACKED, 128)
    left, right = left_tables(), right_tables()
    exchange_buffer = pltpu.VMEM((GROUPS * GROUP_ROWS, 128), f32)
    grid_buffer = pltpu.VMEM((GRID_ROWS, 128), f32)
    dma = pltpu.SemaphoreType.DMA

    def wide(kind):
        return pltpu.VMEM((GUARD + GRID_ROWS, 128), kind)

    out = pl.pallas_call(
        whole_kernel,
        out_shape=jax.ShapeDtypeStruct((PIECES, PARTED, 2, OUT_LOCAL, HALF, 128), f32),
        in_specs=[HBM_SPEC, HBM_SPEC, HBM_SPEC, VMEM_SPEC, SMEM_SPEC, HBM_SPEC, HBM_SPEC],
        out_specs=HBM_SPEC,
        scratch_shapes=[
            pltpu.VMEM((PACKED, 128), jnp.int32),
            pltpu.VMEM((2 * PACKED, 128), bf16),
            pltpu.VMEM((2 * PACKED, 128), f32),
            pltpu.VMEM(potential.shape, f32),
            pltpu.VMEM(left.shape, bf16),
            pltpu.VMEM(right.shape, bf16),
            grid_buffer,
            grid_buffer,
            pltpu.VMEM((GRID_ROWS, 128), jnp.int32),
            wide(f32),
            wide(f32),
            wide(jnp.int32),
        ]
        + [exchange_buffer] * 4
        + [
            pltpu.VMEM((PARTS, 2, 64), f32),
            pltpu.SMEM((PARTS, 2, 64), f32),
            pltpu.VMEM((2 * PACKED, 128), f32),
            pltpu.VMEM((PIECES, BANDS, HALF, 128), f32),
            pltpu.VMEM((PIECES, CHIPS, OUT_LOCAL, HALF, 128), f32),
            dma((5,)),
            dma((2, GROUPS, PARTS)),
            dma((2, GROUPS, PARTS)),
            dma((2, GROUPS)),
            dma((PARTS,)),
            dma((PARTS,)),
            dma((2,)),
        ]
        + [dma((PIECES, CHIPS))] * 2
        + [dma((PIECES,))] * 2
        + [dma((PIECES, CHIPS))] * 2
        + [dma((2, PIECES))],
        compiler_params=pltpu.CompilerParams(
            vmem_limit_bytes=VMEM_BYTES, collective_id=0, has_side_effects=True
        ),
        name="whole",
    )(index, values, potential, rotation, panel_order, jnp.asarray(left), jnp.asarray(right))
    out = out.transpose(3, 0, 1, 2, 4, 5)
    return out.reshape(OUT_LOCAL, PACKED, 2, 128).transpose(0, 2, 1, 3).reshape(OUT_LOCAL, 2, PACKED * 128)


def solution(mesh):
    return jax.shard_map(
        shards,
        mesh=mesh,
        in_specs=(P("band", None, "pw"), P(None, "pw"), P("pw"), P("pw", None), P()),
        out_specs=P("band", None, "pw"),
        check_vma=False,
    )
```
